128 devices in a mesh: bundle: 8 (over z, core), shard: 16 (over x, y).
Axes of the slice: x: 4, y: 4, z: 4, core: 2. Of those that a mesh axis runs over, the one named last changes fastest.
Arguments:
- source: float32 [6, 262144], P(None, ('bundle', 'shard')), may hold values from -4 to 4, as said below
- target: float32 [6, 262144], P(None, ('bundle', 'shard')), may hold values from -4 to 4, as said below
- tile_pairs: int32 [65536, 2], P(('bundle', 'shard')), may hold values from 0 to 2047, as said below
- tile_counts: int32 [128], P(('bundle', 'shard')), may hold values from 1 to 512, as said below
Outputs:
- gradients: float32 [6, 262144], P(None, ('bundle', 'shard'))
The draws below stay inside these ranges and needn't reach their ends.
Inputs may be any that keep to these rules, and one draw needn't show every extreme that they name: `tile_pairs`: row r belongs to owner r // 512 (the device of that index along bundle and shard together). Bundle group g holds blocks g * 128 to g * 128 + 127 of each tractogram. The row block is a source block of the owner's group; a column block q below 1024 is a source block of the same group, and one of 1024 or more is target block q - 1024 of the same or an adjacent group. Slots at or past the owner's count hold valid pairs that are not used. `tile_counts`: entry o is the number of used slots of owner o, counted from its first slot. `source`: every tangent component (rows 3 to 5) has magnitude 0.3 or more. `target`: every tangent component (rows 3 to 5) has magnitude 0.3 or more.
All inputs are finite; a program needn't handle non-finite values.
Results may differ from the reference program's by a relative error of at most 0.0003.
Values sent between devices are 32-bit elements; how exact they have to be, the bound alone decides.
No kernel may reach another device: no remote copies, remote signals or barrier semaphores. Data moves between devices by JAX's collectives and lax.ppermute only.
A program may use at most 64 MiB of HBM per device.

```python
import jax
import jax.numpy as jnp
from jax import lax

B = 256
CAP = 512
NS = 262144
NB = 1024
BPG = 128
N_BUNDLE = 8
N_SHARD = 16
DEVICES = 128


def tangent_rows(key_mag, key_sign):
    magnitude = jax.random.uniform(key_mag, (3, NS), jnp.float32, 0.3, 1.0)
    signs = (jax.random.randint(key_sign, (3, NS), 0, 2) * 2 - 1).astype(jnp.float32)
    return magnitude * signs


def draw_source(key, part):
    key = jax.random.fold_in(key, 3)
    key_pos, key_mag, key_sign = jax.random.split(key, 3)
    centers = jnp.clip(jax.random.normal(key_pos, (3, NS), jnp.float32), -4.0, 4.0)
    return jnp.concatenate([centers, tangent_rows(key_mag, key_sign)], axis=0)


def draw_target(key, part):
    key = jax.random.fold_in(key, 4)
    key_pos, key_mag, key_sign = jax.random.split(key, 3)
    centers = jnp.clip(jax.random.normal(key_pos, (3, NS), jnp.float32), -4.0, 4.0)
    return jnp.concatenate([centers, tangent_rows(key_mag, key_sign)], axis=0)


def draw_tile_pairs(key, part):
    key = jax.random.fold_in(key, 5)
    keys = jax.random.split(key, 4)
    owner_group = (jnp.arange(DEVICES, dtype=jnp.int32) // N_SHARD)[:, None]
    row_block = owner_group * BPG + jax.random.randint(keys[0], (DEVICES, CAP), 0, BPG)
    kind = jax.random.randint(keys[1], (DEVICES, CAP), 0, 4)
    side = jax.random.randint(keys[2], (DEVICES, CAP), 0, 2) * 2 - 1
    beside = owner_group + side
    beside = jnp.where((beside < 0) | (beside >= N_BUNDLE), owner_group - side, beside)
    col_local = jax.random.randint(keys[3], (DEVICES, CAP), 0, BPG)
    target_group = jnp.where(kind == 2, owner_group, beside)
    col_block = jnp.where(kind < 2, owner_group * BPG + col_local, NB + target_group * BPG + col_local)
    col_block = col_block.at[DEVICES - 1, 0].set(2 * NB - 1)
    row_block = row_block.at[0, 0].set(0)
    return jnp.stack([row_block, col_block], axis=-1).reshape(DEVICES * CAP, 2).astype(jnp.int32)


def draw_tile_counts(key, part):
    key = jax.random.fold_in(key, 6)
    keys = jax.random.split(key, 3)
    shift = jax.random.randint(keys[0], (N_BUNDLE, N_SHARD), 1, 4)
    base = jnp.right_shift(jnp.int32(CAP), shift)
    spread = jnp.maximum(jnp.right_shift(jnp.int32(CAP), shift + 2), 1)
    jitter = jax.random.randint(keys[1], (N_BUNDLE, N_SHARD), 0, spread)
    counts = base - jitter
    busiest = jax.random.randint(keys[2], (N_BUNDLE, 1), 0, N_SHARD)
    position = jnp.arange(N_SHARD, dtype=jnp.int32)[None, :]
    counts = jnp.where(position == busiest, CAP, counts)
    return counts.reshape(DEVICES).astype(jnp.int32)


def setup_inputs(seed: int = 0) -> dict:
    splits = jax.random.split(jax.random.key(seed), 5)
    source = draw_source(jax.random.fold_in(splits[4], 71), 0)
    target = draw_target(jax.random.fold_in(splits[4], 71), 0)
    tile_pairs = draw_tile_pairs(jax.random.fold_in(splits[4], 71), 0)
    tile_counts = draw_tile_counts(jax.random.fold_in(splits[4], 71), 0)
    return {"source": source, "target": target, "tile_pairs": tile_pairs, "tile_counts": tile_counts}


kernel_var = 2.0

def tile_gradient(rows, cols, weight):
    centers = rows[0:3]
    tangents = rows[3:6]
    others = cols[0:3]
    other_tan = cols[3:6]
    row_len = jnp.sqrt(lax.optimization_barrier(jnp.sum(tangents * tangents, axis=0)))
    col_len = jnp.sqrt(lax.optimization_barrier(jnp.sum(other_tan * other_tan, axis=0)))
    distance = jnp.zeros((rows.shape[1], rows.shape[2], cols.shape[2]), jnp.float32)
    inner_prod = jnp.zeros((rows.shape[1], rows.shape[2], cols.shape[2]), jnp.float32)
    for axis_a in range(3):
        delta = centers[axis_a][:, :, None] - others[axis_a][:, None, :]
        distance = distance + delta * delta
        inner_prod = inner_prod + tangents[axis_a][:, :, None] * other_tan[axis_a][:, None, :]
    expo = jnp.exp(-distance / kernel_var)
    scale = 1.0 / (row_len[:, :, None] * col_len[:, None, :])
    kernel = expo * inner_prod * inner_prod * scale
    weigh = 2.0 * expo * inner_prod * scale
    row_sum = lax.optimization_barrier(jnp.sum(kernel, axis=2))
    pull = jnp.einsum('tij,atj->ati', kernel, others, precision=lax.Precision.HIGHEST)
    turned = jnp.einsum('tij,atj->ati', weigh, other_tan, precision=lax.Precision.HIGHEST)
    factor = weight[None, :, None]
    grad_pos = factor * (-2.0 / kernel_var) * (centers * row_sum[None] - pull)
    grad_tan = factor * (turned - tangents * (row_sum / (row_len * row_len))[None])
    return jnp.concatenate([grad_pos, grad_tan], axis=0)

def column_slice(array, start):
    return lax.dynamic_slice(array, (jnp.int32(0), start.astype(jnp.int32)), (array.shape[0], B))

def reference(source, target, tile_pairs, tile_counts):

    def owner_step(grads, owner):
        count = tile_counts[owner].astype(jnp.int32)

        def tile_step(slot, grads):
            row_index = (owner.astype(jnp.int32) * CAP + slot.astype(jnp.int32)).astype(jnp.int32)
            pair = lax.dynamic_slice(tile_pairs, (row_index, jnp.int32(0)), (1, 2))[0]
            row_block = pair[0].astype(jnp.int32)
            col_block = pair[1].astype(jnp.int32)
            is_source = col_block < NB
            col_start = (jnp.where(is_source, col_block, col_block - NB) * B).astype(jnp.int32)
            row_start = (row_block * B).astype(jnp.int32)
            rows = column_slice(source, row_start)
            from_src = column_slice(source, col_start)
            from_tgt = column_slice(target, col_start)
            cols = jnp.where(is_source, from_src, from_tgt)
            weight = jnp.where(is_source, jnp.float32(1.0), jnp.float32(-2.0)) / B
            update = tile_gradient(rows[:, None, :], cols[:, None, :], jnp.reshape(weight, (1,)))[:, 0, :]
            current = column_slice(grads, row_start)
            return lax.dynamic_update_slice(grads, current + update, (jnp.int32(0), row_start))
        return (lax.fori_loop(jnp.int32(0), count, tile_step, grads), None)
    start = jnp.zeros((6, NS), jnp.float32)
    grads, unused = lax.scan(owner_step, start, jnp.arange(DEVICES, dtype=jnp.int32))
    return grads
```

```python
import functools

import jax
import jax.numpy as jnp
from jax import lax
from jax.experimental import pallas as pl
from jax.experimental.pallas import tpu as pltpu
from jax.sharding import PartitionSpec as P

B = 256
LANES = 128
PAYLOAD = 32
LOG2E = 1.4426950408889634
SENDERS = 16
SPLIT = 4
ARRAYS = 4
KEXP = 32
FEATS = 24
ROWS = 2 * SENDERS
COLS = ARRAYS * ROWS
UNROLL = 2
VMEM_LIMIT = 50 * 1024 * 1024

NT = (((1,), (1,)), ((), ()))


def split3(value):
    first = value.astype(jnp.bfloat16).astype(jnp.float32)
    rest = value - first
    second = rest.astype(jnp.bfloat16).astype(jnp.float32)
    return first, second, rest - second


def sort_kernel(count_ref, pairs_ref, lists_ref):
    slots = pairs_ref.shape[1]
    group = lax.axis_index("bundle")
    row = pairs_ref[0:1, :]
    col = pairs_ref[1:2, :]
    total_blocks = 8 * 128
    row_local = row - group * 128
    is_source = col < total_blocks
    shifted = col - jnp.where(is_source, group * 128, total_blocks + (group - 1) * 128)
    array = jnp.where(is_source, 0, 1 + lax.shift_right_arithmetic(shifted, 7))
    col_local = lax.bitwise_and(shifted, 127)
    rclass = lax.bitwise_and(lax.shift_right_logical(row_local, 1), 3)
    cclass = lax.bitwise_and(lax.shift_right_logical(col_local, 1), 3)
    rindex = 2 * lax.shift_right_logical(row_local, 3) + lax.bitwise_and(row_local, 1)
    cindex = 32 * array + 2 * lax.shift_right_logical(col_local, 3) + lax.bitwise_and(col_local, 1)
    live = lax.broadcasted_iota(jnp.int32, (1, slots), 1) < count_ref[0]
    dest = jnp.where(live, rclass * SPLIT + cclass, 1000)

    lane = lax.broadcasted_iota(jnp.int32, (slots, slots), 1)
    sub = lax.broadcasted_iota(jnp.int32, (slots, slots), 0)
    earlier = (sub < lane).astype(jnp.float32).astype(jnp.bfloat16)
    owner = lax.broadcasted_iota(jnp.int32, (SENDERS, slots), 0)
    mine = (owner == dest).astype(jnp.float32)
    rank = jnp.dot(mine.astype(jnp.bfloat16), earlier, preferred_element_type=jnp.float32)
    below = (lax.broadcasted_iota(jnp.int32, (128, slots), 0) > dest).astype(jnp.float32)
    start = jnp.sum(below[0:SENDERS], axis=1, keepdims=True)
    place = jnp.sum(mine * (rank + start), axis=0, keepdims=True).astype(jnp.int32)
    place = jnp.where(live, place, -1)
    onehot = (sub == place).astype(jnp.float32).astype(jnp.bfloat16)
    zero = jnp.zeros((6, slots), jnp.float32)
    halves = jnp.concatenate([rindex.astype(jnp.float32), cindex.astype(jnp.float32), zero], axis=0)
    moved = lax.dot_general(halves.astype(jnp.bfloat16), onehot, NT, preferred_element_type=jnp.float32)
    offsets = lax.dot_general(
        jnp.ones((8, slots), jnp.bfloat16), below.astype(jnp.bfloat16), NT, preferred_element_type=jnp.float32
    )
    lists_ref[0:1, :] = moved[0:1] * 128.0 + moved[1:2]
    lists_ref[1:2, :] = jnp.concatenate([offsets[0:1], jnp.zeros((1, slots - 128), jnp.float32)], axis=1)


def pack_kernel(src_ref, before_ref, tgt_ref, after_ref, lists_ref, out_ref):
    for j in range(SPLIT):
        for tile in range(SPLIT):
            part = pl.ds((j * SPLIT + tile) * LANES, LANES)
            cols = jnp.concatenate(
                [
                    src_ref[:, part],
                    before_ref[:, part],
                    tgt_ref[:, part],
                    after_ref[:, part],
                    lists_ref[:, tile * LANES:(tile + 1) * LANES],
                ],
                axis=0,
            )
            rows = src_ref[:, part]
            for i in range(SPLIT):
                out_ref[i * SPLIT + j, tile, 6:PAYLOAD, :] = cols
                out_ref[j * SPLIT + i, tile, 0:6, :] = rows


def tile_kernel(
    recv_ref, out_ref, index_ref, lists_ref, flat_ref, colb_ref, colf_ref, rowa_ref, bexp_ref, feat_ref, aexp_ref,
    acc_ref, sem,
):
    me = lax.axis_index("shard")

    def take(row, tile):
        return recv_ref[pl.ds(tile * PAYLOAD + row, SENDERS, stride=SPLIT * PAYLOAD), :]

    for tile in range(SPLIT):
        index_ref[tile * SENDERS:(tile + 1) * SENDERS, :] = take(30, tile).astype(jnp.int32)
    index_ref[SPLIT * SENDERS:(SPLIT + 1) * SENDERS, :] = take(31, 0).astype(jnp.int32)
    copy = pltpu.make_async_copy(index_ref, lists_ref, sem)
    copy.start()

    one = jnp.ones((SENDERS, LANES), jnp.float32)
    nil = jnp.zeros((SENDERS, LANES), jnp.float32)
    order_row = (0, 0, 1, 1, 0, 2)
    order_col = (0, 1, 0, 1, 2, 0)
    pairs = ((0, 0), (0, 1), (0, 2), (1, 1), (1, 2), (2, 2))

    for tile in range(SPLIT):
        half, side = divmod(tile, 2)

        def put(ref, count, first, height, row, value):
            start = (side * count + first + half) * height + row
            ref[pl.ds(start, SENDERS, stride=2 * height), :] = value

        center = [take(a, tile) for a in range(3)]
        norm = (center[0] * center[0] + center[1] * center[1] + center[2] * center[2]) * (-0.5 * LOG2E)
        parts = [split3(c * LOG2E) for c in center]
        norms = split3(norm)
        for k, level in enumerate(order_row):
            for a in range(3):
                put(rowa_ref, ROWS, 0, KEXP, 3 * k + a, parts[a][level])
        for k in range(3):
            put(rowa_ref, ROWS, 0, KEXP, 18 + k, norms[k])
            put(rowa_ref, ROWS, 0, KEXP, 21 + k, one)
        for k in range(24, KEXP):
            put(rowa_ref, ROWS, 0, KEXP, k, nil)

        for array in range(ARRAYS):
            base = 6 + 6 * array
            first = array * ROWS
            center = [take(base + a, tile) for a in range(3)]
            tangent = [take(base + 3 + a, tile) for a in range(3)]
            norm = (center[0] * center[0] + center[1] * center[1] + center[2] * center[2]) * (-0.5 * LOG2E)
            parts = [split3(c) for c in center]
            norms = split3(norm)
            for k, level in enumerate(order_col):
                for a in range(3):
                    put(colb_ref, COLS, first, KEXP, 3 * k + a, parts[a][level])
            for k in range(3):
                put(colb_ref, COLS, first, KEXP, 18 + k, one)
                put(colb_ref, COLS, first, KEXP, 21 + k, norms[k])
            for k in range(24, KEXP):
                put(colb_ref, COLS, first, KEXP, k, nil)
            square = tangent[0] * tangent[0] + tangent[1] * tangent[1] + tangent[2] * tangent[2]
            scale = (1.0 if array == 0 else -2.0) / jnp.sqrt(square)
            for n, (a, b) in enumerate(pairs):
                moment = tangent[a] * tangent[b] * scale
                put(colf_ref, COLS, first, FEATS, n, moment)
                for c in range(3):
                    put(colf_ref, COLS, first, FEATS, 6 * (c + 1) + n, moment * center[c])

    def both(ref, count, block, height):
        return jnp.concatenate(
            [ref[pl.ds(pl.multiple_of((side * count + block) * height, 8), height), :] for side in range(2)], axis=1
        )

    def row_block(block, carry):
        aexp_ref[block] = both(rowa_ref, ROWS, block, KEXP).T.astype(jnp.bfloat16)
        return carry

    lax.fori_loop(0, ROWS, row_block, 0)
    acc_ref[...] = jnp.zeros(acc_ref.shape, jnp.float32)

    def col_block(block, carry):
        bexp_ref[block] = both(colb_ref, COLS, block, KEXP).astype(jnp.bfloat16)
        feats = both(colf_ref, COLS, block, FEATS)
        high = feats.astype(jnp.bfloat16).astype(jnp.float32)
        feat_ref[block] = jnp.concatenate([high, feats - high], axis=0).astype(jnp.bfloat16)
        return carry

    lax.fori_loop(0, COLS, col_block, 0)
    bexp_ref[COLS] = jnp.zeros((KEXP, B), jnp.bfloat16)
    feat_ref[COLS] = jnp.zeros((2 * FEATS, B), jnp.bfloat16)

    copy.wait()

    def sender(s, total):
        low = lists_ref[SPLIT * SENDERS + s, me]
        high = lists_ref[SPLIT * SENDERS + s, me + 1]

        def move(k, total):
            flat_ref[total] = lists_ref[lax.shift_right_logical(k, 7) * SENDERS + s, lax.bitwise_and(k, 127)]
            return total + 1

        return lax.fori_loop(low, high, move, total)

    total = lax.fori_loop(0, SENDERS, sender, jnp.int32(0))
    for k in range(UNROLL):
        flat_ref[total + k] = jnp.int32(-1)

    def turn(step, carry):
        for k in range(UNROLL):
            code = flat_ref[step * UNROLL + k]
            dead = code < 0
            r = jnp.where(dead, 0, lax.shift_right_logical(code, 7))
            q = jnp.where(dead, COLS, lax.bitwise_and(code, 127))
            expo = jnp.dot(aexp_ref[r], bexp_ref[q], preferred_element_type=jnp.float32)
            value = jnp.exp2(expo)
            high = value.astype(jnp.bfloat16)
            low = (value - high.astype(jnp.float32)).astype(jnp.bfloat16)
            feats = feat_ref[q]
            got = lax.dot_general(feats, high, NT, preferred_element_type=jnp.float32)
            got += lax.dot_general(feats, low, NT, preferred_element_type=jnp.float32)
            for side in range(2):
                part = pl.ds(pl.multiple_of((side * ROWS + r) * 2 * FEATS, 8), 2 * FEATS)
                acc_ref[part, :] += got[:, side * LANES:(side + 1) * LANES]
        return carry

    lax.fori_loop(0, lax.div(total + (UNROLL - 1), UNROLL), turn, 0)

    for tile in range(SPLIT):
        half, side = divmod(tile, 2)
        center = [take(a, tile) for a in range(3)]
        tangent = [take(3 + a, tile) for a in range(3)]

        def moment(f):
            start = (side * ROWS + half) * 2 * FEATS + f
            stride = 4 * FEATS
            return acc_ref[pl.ds(start, SENDERS, stride=stride), :] + acc_ref[
                pl.ds(start + FEATS, SENDERS, stride=stride), :
            ]

        square = tangent[0] * tangent[0] + tangent[1] * tangent[1] + tangent[2] * tangent[2]
        inverse = 1.0 / jnp.sqrt(square)
        place = {}
        for n, (a, b) in enumerate(pairs):
            place[a, b] = place[b, a] = n

        def form(offset):
            m = [moment(offset + n) for n in range(6)]
            y = [
                m[place[a, 0]] * tangent[0] + m[place[a, 1]] * tangent[1] + m[place[a, 2]] * tangent[2]
                for a in range(3)
            ]
            return y, (y[0] * tangent[0] + y[1] * tangent[1] + y[2] * tangent[2]) * inverse

        def emit(row, value):
            out_ref[pl.ds(tile * 6 + row, SENDERS, stride=SPLIT * 6), :] = value * (1.0 / B)

        turned, total_k = form(0)
        ratio = total_k / square
        for a in range(3):
            _, pull = form(6 * (a + 1))
            emit(a, pull - center[a] * total_k)
            emit(3 + a, 2.0 * inverse * turned[a] - tangent[a] * ratio)


def per_device(source, target, tile_pairs, tile_counts):
    groups = lax.axis_size("bundle")
    up = [(i, i + 1) for i in range(groups - 1)]
    down = [(i + 1, i) for i in range(groups - 1)]
    before = lax.ppermute(target, "bundle", up)
    after = lax.ppermute(target, "bundle", down)
    vmem = pl.BlockSpec(memory_space=pltpu.VMEM)
    params = pltpu.CompilerParams(vmem_limit_bytes=VMEM_LIMIT)
    slots = tile_pairs.shape[0]
    lists = pl.pallas_call(
        sort_kernel,
        out_shape=jax.ShapeDtypeStruct((2, slots), jnp.float32),
        in_specs=[pl.BlockSpec(memory_space=pltpu.SMEM), vmem],
        out_specs=vmem,
        compiler_params=params,
        name="sort_tiles",
    )(tile_counts, tile_pairs.T)
    send = pl.pallas_call(
        pack_kernel,
        out_shape=jax.ShapeDtypeStruct((SENDERS, SPLIT, PAYLOAD, LANES), jnp.float32),
        in_specs=[vmem] * 5,
        out_specs=vmem,
        compiler_params=params,
        name="pack",
    )(source, before, target, after, lists)
    recv = lax.all_to_all(send, "shard", split_axis=0, concat_axis=0, tiled=True)
    partial = tiles(recv).reshape(SENDERS, SPLIT * 6, LANES)
    back = lax.all_to_all(partial, "shard", split_axis=0, concat_axis=0, tiled=True)
    return pl.pallas_call(
        sum_kernel,
        out_shape=jax.ShapeDtypeStruct((6, 8 * B), jnp.float32),
        in_specs=[vmem],
        out_specs=vmem,
        compiler_params=params,
        name="add_parts",
    )(back)


def sum_kernel(back_ref, out_ref):
    for i in range(SPLIT):
        parts = [back_ref[i * SPLIT + j] for j in range(SPLIT)]
        total = (parts[0] + parts[1]) + (parts[2] + parts[3])
        for tile in range(SPLIT):
            part = pl.ds((i * SPLIT + tile) * LANES, LANES)
            out_ref[:, part] = total[tile * 6:(tile + 1) * 6, :]


def tiles(recv):
    vmem = pl.BlockSpec(memory_space=pltpu.VMEM)
    return pl.pallas_call(
        tile_kernel,
        out_shape=jax.ShapeDtypeStruct((SENDERS * SPLIT * 6, LANES), jnp.float32),
        in_specs=[vmem],
        out_specs=vmem,
        scratch_shapes=[
            pltpu.VMEM(((SPLIT + 1) * SENDERS, LANES), jnp.int32),
            pltpu.SMEM(((SPLIT + 1) * SENDERS, LANES), jnp.int32),
            pltpu.SMEM((SENDERS * 512 + 128,), jnp.int32),
            pltpu.VMEM((2 * COLS * KEXP, LANES), jnp.float32),
            pltpu.VMEM((2 * COLS * FEATS, LANES), jnp.float32),
            pltpu.VMEM((2 * ROWS * KEXP, LANES), jnp.float32),
            pltpu.VMEM((COLS + 1, KEXP, B), jnp.bfloat16),
            pltpu.VMEM((COLS + 1, 2 * FEATS, B), jnp.bfloat16),
            pltpu.VMEM((ROWS, B, KEXP), jnp.bfloat16),
            pltpu.VMEM((2 * ROWS * 2 * FEATS, LANES), jnp.float32),
            pltpu.SemaphoreType.DMA,
        ],
        compiler_params=pltpu.CompilerParams(vmem_limit_bytes=VMEM_LIMIT),
        name="tile_gradients",
    )(recv.reshape(SENDERS * SPLIT * PAYLOAD, LANES))


def solution(mesh):
    in_specs = (
        P(None, ("bundle", "shard")),
        P(None, ("bundle", "shard")),
        P(("bundle", "shard"), None),
        P(("bundle", "shard")),
    )
    out_specs = P(None, ("bundle", "shard"))
    return jax.shard_map(
        per_device, mesh=mesh, in_specs=in_specs, out_specs=out_specs, check_vma=False
    )
```

```python
import functools

import jax
import jax.numpy as jnp
from jax import lax
from jax.experimental import pallas as pl
from jax.experimental.pallas import tpu as pltpu
from jax.sharding import PartitionSpec as P

B = 256
LANES = 128
PAYLOAD = 32
LOG2E = 1.4426950408889634
SENDERS = 16
SPLIT = 4
ARRAYS = 4
KEXP = 32
KPITCH = 33
FEATS = 24
FPITCH = 25
APITCH = 49
ROWS = 2 * SENDERS
COLS = ARRAYS * ROWS
UNROLL = 8
VMEM_LIMIT = 50 * 1024 * 1024

NT = (((1,), (1,)), ((), ()))


def split3(value):
    first = value.astype(jnp.bfloat16).astype(jnp.float32)
    rest = value - first
    second = rest.astype(jnp.bfloat16).astype(jnp.float32)
    return first, second, rest - second


def sort_kernel(count_ref, pairs_ref, lists_ref):
    slots = pairs_ref.shape[1]
    group = lax.axis_index("bundle")
    row = pairs_ref[0:1, :]
    col = pairs_ref[1:2, :]
    total_blocks = 8 * 128
    row_local = row - group * 128
    is_source = col < total_blocks
    shifted = col - jnp.where(is_source, group * 128, total_blocks + (group - 1) * 128)
    array = jnp.where(is_source, 0, 1 + lax.shift_right_arithmetic(shifted, 7))
    col_local = lax.bitwise_and(shifted, 127)
    rclass = lax.bitwise_and(lax.shift_right_logical(row_local, 1), 3)
    cclass = lax.bitwise_and(lax.shift_right_logical(col_local, 1), 3)
    rindex = lax.shift_right_logical(row_local, 3) + 16 * lax.bitwise_and(row_local, 1)
    cindex = 32 * array + lax.shift_right_logical(col_local, 3) + 16 * lax.bitwise_and(col_local, 1)
    live = lax.broadcasted_iota(jnp.int32, (1, slots), 1) < count_ref[0]
    dest = jnp.where(live, rclass * SPLIT + cclass, 1000)

    lane = lax.broadcasted_iota(jnp.int32, (slots, slots), 1)
    sub = lax.broadcasted_iota(jnp.int32, (slots, slots), 0)
    earlier = (sub < lane).astype(jnp.float32).astype(jnp.bfloat16)
    owner = lax.broadcasted_iota(jnp.int32, (SENDERS, slots), 0)
    mine = (owner == dest).astype(jnp.float32)
    rank = jnp.dot(mine.astype(jnp.bfloat16), earlier, preferred_element_type=jnp.float32)
    below = (lax.broadcasted_iota(jnp.int32, (128, slots), 0) > dest).astype(jnp.float32)
    start = jnp.sum(below[0:SENDERS], axis=1, keepdims=True)
    place = jnp.sum(mine * (rank + start), axis=0, keepdims=True).astype(jnp.int32)
    place = jnp.where(live, place, -1)
    onehot = (sub == place).astype(jnp.float32).astype(jnp.bfloat16)
    zero = jnp.zeros((6, slots), jnp.float32)
    halves = jnp.concatenate([rindex.astype(jnp.float32), cindex.astype(jnp.float32), zero], axis=0)
    moved = lax.dot_general(halves.astype(jnp.bfloat16), onehot, NT, preferred_element_type=jnp.float32)
    offsets = lax.dot_general(
        jnp.ones((8, slots), jnp.bfloat16), below.astype(jnp.bfloat16), NT, preferred_element_type=jnp.float32
    )
    lists_ref[0:1, :] = moved[0:1] * 128.0 + moved[1:2]
    lists_ref[1:2, :] = jnp.concatenate([offsets[0:1], jnp.zeros((1, slots - 128), jnp.float32)], axis=1)


def pack_kernel(src_ref, before_ref, tgt_ref, after_ref, lists_ref, out_ref):
    for j in range(SPLIT):
        for tile in range(SPLIT):
            part = pl.ds((j * SPLIT + tile) * LANES, LANES)
            cols = jnp.concatenate(
                [
                    src_ref[:, part],
                    before_ref[:, part],
                    tgt_ref[:, part],
                    after_ref[:, part],
                    lists_ref[:, tile * LANES:(tile + 1) * LANES],
                ],
                axis=0,
            )
            rows = src_ref[:, part]
            for i in range(SPLIT):
                out_ref[i * SPLIT + j, tile, 6:PAYLOAD, :] = cols
                out_ref[j * SPLIT + i, tile, 0:6, :] = rows


def tile_kernel(
    recv_ref, out_ref, index_ref, lists_ref, flat_ref, colb_ref, colf_ref, rowa_ref, aexp_ref, acc_ref, sem,
):
    me = lax.axis_index("shard")

    def take(row, tile):
        return recv_ref[pl.ds(tile * PAYLOAD + row, SENDERS, stride=SPLIT * PAYLOAD), :]

    for tile in range(SPLIT):
        index_ref[tile * SENDERS:(tile + 1) * SENDERS, :] = take(30, tile).astype(jnp.int32)
    index_ref[SPLIT * SENDERS:(SPLIT + 1) * SENDERS, :] = take(31, 0).astype(jnp.int32)
    copy = pltpu.make_async_copy(index_ref, lists_ref, sem)
    copy.start()

    one = jnp.ones((SENDERS, LANES), jnp.float32)
    nil = jnp.zeros((SENDERS, LANES), jnp.float32)
    order_row = (0, 0, 1, 1, 0, 2)
    order_col = (0, 1, 0, 1, 2, 0)
    pairs = ((0, 0), (0, 1), (0, 2), (1, 1), (1, 2), (2, 2))

    for tile in range(SPLIT):
        half, side = divmod(tile, 2)

        def put(ref, count, first, height, row, value):
            start = (side * count + first + half * SENDERS) * height + row
            ref[pl.ds(start, SENDERS, stride=height), :] = value

        center = [take(a, tile) for a in range(3)]
        norm = (center[0] * center[0] + center[1] * center[1] + center[2] * center[2]) * (-0.5 * LOG2E)
        parts = [split3(c * LOG2E) for c in center]
        norms = split3(norm)
        for k, level in enumerate(order_row):
            for a in range(3):
                put(rowa_ref, ROWS, 0, KPITCH, 3 * k + a, parts[a][level])
        for k in range(3):
            put(rowa_ref, ROWS, 0, KPITCH, 18 + k, norms[k])
            put(rowa_ref, ROWS, 0, KPITCH, 21 + k, one)
        for k in range(24, KEXP):
            put(rowa_ref, ROWS, 0, KPITCH, k, nil)

        for array in range(ARRAYS):
            base = 6 + 6 * array
            first = array * ROWS
            center = [take(base + a, tile) for a in range(3)]
            tangent = [take(base + 3 + a, tile) for a in range(3)]
            norm = (center[0] * center[0] + center[1] * center[1] + center[2] * center[2]) * (-0.5 * LOG2E)
            parts = [split3(c) for c in center]
            norms = split3(norm)
            for k, level in enumerate(order_col):
                for a in range(3):
                    put(colb_ref, COLS + 1, first, KPITCH, 3 * k + a, parts[a][level])
            for k in range(3):
                put(colb_ref, COLS + 1, first, KPITCH, 18 + k, one)
                put(colb_ref, COLS + 1, first, KPITCH, 21 + k, norms[k])
            for k in range(24, KEXP):
                put(colb_ref, COLS + 1, first, KPITCH, k, nil)
            square = tangent[0] * tangent[0] + tangent[1] * tangent[1] + tangent[2] * tangent[2]
            scale = (1.0 if array == 0 else -2.0) / jnp.sqrt(square)
            for n, (a, b) in enumerate(pairs):
                moment = tangent[a] * tangent[b] * scale
                put(colf_ref, COLS + 1, first, FPITCH, n, moment)
                for c in range(3):
                    put(colf_ref, COLS + 1, first, FPITCH, 6 * (c + 1) + n, moment * center[c])

    for side in range(2):
        blank = ((side + 1) * (COLS + 1) - 1)
        colb_ref[blank * KPITCH:blank * KPITCH + KEXP, :] = jnp.zeros((KEXP, LANES), jnp.float32)
        colf_ref[blank * FPITCH:blank * FPITCH + FEATS, :] = jnp.zeros((FEATS, LANES), jnp.float32)
    acc_ref[...] = jnp.zeros(acc_ref.shape, jnp.float32)

    def both(ref, count, block, pitch, height):
        return jnp.concatenate(
            [ref[pl.ds((side * count + block) * pitch, height), :] for side in range(2)], axis=1
        )

    for block in range(ROWS):
        aexp_ref[block] = both(rowa_ref, ROWS, block, KPITCH, KEXP).astype(jnp.bfloat16)

    copy.wait()

    def sender(s, total):
        low = lists_ref[SPLIT * SENDERS + s, me]
        high = lists_ref[SPLIT * SENDERS + s, me + 1]

        def move(k, total):
            flat_ref[total] = lists_ref[lax.shift_right_logical(k, 7) * SENDERS + s, lax.bitwise_and(k, 127)]
            return total + 1

        return lax.fori_loop(low, high, move, total)

    total = lax.fori_loop(0, SENDERS, sender, jnp.int32(0))
    for k in range(UNROLL):
        flat_ref[total + k] = jnp.int32(-1)

    def turn(step, carry):
        for k in range(UNROLL):
            code = flat_ref[step * UNROLL + k]
            dead = code < 0
            r = jnp.where(dead, 0, lax.shift_right_logical(code, 7))
            q = jnp.where(dead, COLS, lax.bitwise_and(code, 127))
            turned = both(colb_ref, COLS + 1, q, KPITCH, KEXP).T.astype(jnp.bfloat16)
            expo = jnp.dot(turned, aexp_ref[r], preferred_element_type=jnp.float32)
            value = jnp.exp2(expo)
            high = value.astype(jnp.bfloat16)
            low = (value - high.astype(jnp.float32)).astype(jnp.bfloat16)
            feats = both(colf_ref, COLS + 1, q, FPITCH, FEATS)
            upper = feats.astype(jnp.bfloat16).astype(jnp.float32)
            feats = jnp.concatenate([upper, feats - upper], axis=0).astype(jnp.bfloat16)
            got = jnp.dot(feats, high, preferred_element_type=jnp.float32)
            got += jnp.dot(feats, low, preferred_element_type=jnp.float32)
            for side in range(2):
                part = pl.ds((side * ROWS + r) * APITCH, 2 * FEATS)
                acc_ref[part, :] += got[:, side * LANES:(side + 1) * LANES]
        return carry

    lax.fori_loop(0, lax.div(total + (UNROLL - 1), UNROLL), turn, 0)

    for tile in range(SPLIT):
        half, side = divmod(tile, 2)
        center = [take(a, tile) for a in range(3)]
        tangent = [take(3 + a, tile) for a in range(3)]

        def moment(f):
            start = (side * ROWS + half * SENDERS) * APITCH + f
            return acc_ref[pl.ds(start, SENDERS, stride=APITCH), :] + acc_ref[
                pl.ds(start + FEATS, SENDERS, stride=APITCH), :
            ]

        square = tangent[0] * tangent[0] + tangent[1] * tangent[1] + tangent[2] * tangent[2]
        inverse = 1.0 / jnp.sqrt(square)
        place = {}
        for n, (a, b) in enumerate(pairs):
            place[a, b] = place[b, a] = n

        def form(offset):
            m = [moment(offset + n) for n in range(6)]
            y = [
                m[place[a, 0]] * tangent[0] + m[place[a, 1]] * tangent[1] + m[place[a, 2]] * tangent[2]
                for a in range(3)
            ]
            return y, (y[0] * tangent[0] + y[1] * tangent[1] + y[2] * tangent[2]) * inverse

        def emit(row, value):
            out_ref[pl.ds(tile * 6 + row, SENDERS, stride=SPLIT * 6), :] = value * (1.0 / B)

        turned, total_k = form(0)
        ratio = total_k / square
        for a in range(3):
            _, pull = form(6 * (a + 1))
            emit(a, pull - center[a] * total_k)
            emit(3 + a, 2.0 * inverse * turned[a] - tangent[a] * ratio)


def per_device(source, target, tile_pairs, tile_counts):
    groups = lax.axis_size("bundle")
    up = [(i, i + 1) for i in range(groups - 1)]
    down = [(i + 1, i) for i in range(groups - 1)]
    before = lax.ppermute(target, "bundle", up)
    after = lax.ppermute(target, "bundle", down)
    vmem = pl.BlockSpec(memory_space=pltpu.VMEM)
    params = pltpu.CompilerParams(vmem_limit_bytes=VMEM_LIMIT)
    slots = tile_pairs.shape[0]
    lists = pl.pallas_call(
        sort_kernel,
        out_shape=jax.ShapeDtypeStruct((2, slots), jnp.float32),
        in_specs=[pl.BlockSpec(memory_space=pltpu.SMEM), vmem],
        out_specs=vmem,
        compiler_params=params,
        name="sort_tiles",
    )(tile_counts, tile_pairs.T)
    send = pl.pallas_call(
        pack_kernel,
        out_shape=jax.ShapeDtypeStruct((SENDERS, SPLIT, PAYLOAD, LANES), jnp.float32),
        in_specs=[vmem] * 5,
        out_specs=vmem,
        compiler_params=params,
        name="pack",
    )(source, before, target, after, lists)
    recv = lax.all_to_all(send, "shard", split_axis=0, concat_axis=0, tiled=True)
    partial = tiles(recv).reshape(SENDERS, SPLIT * 6, LANES)
    back = lax.all_to_all(partial, "shard", split_axis=0, concat_axis=0, tiled=True)
    return pl.pallas_call(
        sum_kernel,
        out_shape=jax.ShapeDtypeStruct((6, 8 * B), jnp.float32),
        in_specs=[vmem],
        out_specs=vmem,
        compiler_params=params,
        name="add_parts",
    )(back)


def sum_kernel(back_ref, out_ref):
    for i in range(SPLIT):
        parts = [back_ref[i * SPLIT + j] for j in range(SPLIT)]
        total = (parts[0] + parts[1]) + (parts[2] + parts[3])
        for tile in range(SPLIT):
            part = pl.ds((i * SPLIT + tile) * LANES, LANES)
            out_ref[:, part] = total[tile * 6:(tile + 1) * 6, :]


def tiles(recv):
    vmem = pl.BlockSpec(memory_space=pltpu.VMEM)
    return pl.pallas_call(
        tile_kernel,
        out_shape=jax.ShapeDtypeStruct((SENDERS * SPLIT * 6, LANES), jnp.float32),
        in_specs=[vmem],
        out_specs=vmem,
        scratch_shapes=[
            pltpu.VMEM(((SPLIT + 1) * SENDERS, LANES), jnp.int32),
            pltpu.SMEM(((SPLIT + 1) * SENDERS, LANES), jnp.int32),
            pltpu.SMEM((SENDERS * 512 + 128,), jnp.int32),
            pltpu.VMEM((2 * (COLS + 1) * KPITCH, LANES), jnp.float32),
            pltpu.VMEM((2 * (COLS + 1) * FPITCH, LANES), jnp.float32),
            pltpu.VMEM((2 * ROWS * KPITCH, LANES), jnp.float32),
            pltpu.VMEM((ROWS, KEXP, B), jnp.bfloat16),
            pltpu.VMEM((2 * ROWS * APITCH, LANES), jnp.float32),
            pltpu.SemaphoreType.DMA,
        ],
        compiler_params=pltpu.CompilerParams(vmem_limit_bytes=VMEM_LIMIT),
        name="tile_gradients",
    )(recv.reshape(SENDERS * SPLIT * PAYLOAD, LANES))


def solution(mesh):
    in_specs = (
        P(None, ("bundle", "shard")),
        P(None, ("bundle", "shard")),
        P(("bundle", "shard"), None),
        P(("bundle", "shard")),
    )
    out_specs = P(None, ("bundle", "shard"))
    return jax.shard_map(
        per_device, mesh=mesh, in_specs=in_specs, out_specs=out_specs, check_vma=False
    )
```

```python
import functools

import jax
import jax.numpy as jnp
from jax import lax
from jax.experimental import pallas as pl
from jax.experimental.pallas import tpu as pltpu
from jax.sharding import PartitionSpec as P

B = 256
LANES = 128
PAYLOAD = 32
LOG2E = 1.4426950408889634
SENDERS = 16
SPLIT = 4
ARRAYS = 4
KEXP = 32
KPITCH = 33
FEATS = 24
FPITCH = 25
APITCH = 49
ROWS = 2 * SENDERS
COLS = ARRAYS * ROWS
UNROLL = 32
TAIL = 16
BASES = (6, 18, 12, 24)
VMEM_LIMIT = 40 * 1024 * 1024

NT = (((1,), (1,)), ((), ()))


def split3(value):
    first = value.astype(jnp.bfloat16).astype(jnp.float32)
    rest = value - first
    second = rest.astype(jnp.bfloat16).astype(jnp.float32)
    return first, second, rest - second


def own_kernel(count_ref, pairs_hbm, src_hbm, tgt_hbm, out_ref, pairs_ref, src_ref, tgt_ref, lists_ref, sems):
    copies = [
        pltpu.make_async_copy(source, target, sems.at[n])
        for n, (source, target) in enumerate(((pairs_hbm, pairs_ref), (src_hbm, src_ref), (tgt_hbm, tgt_ref)))
    ]
    for copy in copies:
        copy.start()
    copies[0].wait()
    sort_tiles(count_ref, pairs_ref, lists_ref)
    copies[1].wait()
    copies[2].wait()
    for j in range(SPLIT):
        for tile in range(SPLIT):
            part = pl.ds((j * SPLIT + tile) * LANES, LANES)
            rows = src_ref[:, part]
            cols = jnp.concatenate([rows, tgt_ref[:, part]], axis=0)
            lists = lists_ref[:, tile * LANES:(tile + 1) * LANES]
            for i in range(SPLIT):
                out_ref[i * SPLIT + j, tile, 6:18, :] = cols
                out_ref[i * SPLIT + j, tile, 30:32, :] = lists
                out_ref[j * SPLIT + i, tile, 0:6, :] = rows


def halo_kernel(own_ref, before_ref, after_ref, out_ref):
    del own_ref
    for j in range(SPLIT):
        for tile in range(SPLIT):
            part = pl.ds((j * SPLIT + tile) * LANES, LANES)
            cols = jnp.concatenate([before_ref[:, part], after_ref[:, part]], axis=0)
            for i in range(SPLIT):
                out_ref[i * SPLIT + j, tile, 18:30, :] = cols


def sort_tiles(count_ref, pairs_ref, lists_ref):
    slots = pairs_ref.shape[1]
    group = lax.axis_index("bundle")
    row = pairs_ref[0:1, :]
    col = pairs_ref[1:2, :]
    total_blocks = 8 * 128
    row_local = row - group * 128
    is_source = col < total_blocks
    shifted = col - jnp.where(is_source, group * 128, total_blocks + (group - 1) * 128)
    step = 1 + lax.shift_right_arithmetic(shifted, 7)
    step = jnp.where(lax.bitwise_and(group, 1) == 1, step, 4 - step)
    array = jnp.where(is_source, 0, step)
    col_local = lax.bitwise_and(shifted, 127)
    rclass = lax.bitwise_and(lax.shift_right_logical(row_local, 1), 3)
    cclass = lax.bitwise_and(lax.shift_right_logical(col_local, 1), 3)
    rindex = lax.shift_right_logical(row_local, 3) + 16 * lax.bitwise_and(row_local, 1)
    cindex = 32 * array + lax.shift_right_logical(col_local, 3) + 16 * lax.bitwise_and(col_local, 1)
    live = lax.broadcasted_iota(jnp.int32, (1, slots), 1) < count_ref[0]
    dest = jnp.where(live, rclass * SPLIT + cclass, 1000)

    lane = lax.broadcasted_iota(jnp.int32, (slots, slots), 1)
    sub = lax.broadcasted_iota(jnp.int32, (slots, slots), 0)
    earlier = (sub < lane).astype(jnp.float32).astype(jnp.bfloat16)
    owner = lax.broadcasted_iota(jnp.int32, (SENDERS, slots), 0)
    mine = (owner == dest).astype(jnp.float32)
    rank = jnp.dot(mine.astype(jnp.bfloat16), earlier, preferred_element_type=jnp.float32)
    below = (lax.broadcasted_iota(jnp.int32, (128, slots), 0) > dest).astype(jnp.float32)
    start = jnp.sum(below[0:SENDERS], axis=1, keepdims=True)
    place = jnp.sum(mine * (rank + start), axis=0, keepdims=True).astype(jnp.int32)
    place = jnp.where(live, place, -1)
    onehot = (sub == place).astype(jnp.float32).astype(jnp.bfloat16)
    zero = jnp.zeros((6, slots), jnp.float32)
    halves = jnp.concatenate([rindex.astype(jnp.float32), cindex.astype(jnp.float32), zero], axis=0)
    moved = lax.dot_general(halves.astype(jnp.bfloat16), onehot, NT, preferred_element_type=jnp.float32)
    offsets = lax.dot_general(
        jnp.ones((8, slots), jnp.bfloat16), below.astype(jnp.bfloat16), NT, preferred_element_type=jnp.float32
    )
    lists_ref[0:1, :] = moved[0:1] * 128.0 + moved[1:2]
    lists_ref[1:2, :] = jnp.concatenate([offsets[0:1], jnp.zeros((1, slots - 128), jnp.float32)], axis=1)


def tile_kernel(
    recv_ref, out_ref, index_ref, lists_ref, flat_ref, colb_ref, colf_ref, rowa_ref, aexp_ref, acc_ref, sem,
):
    me = lax.axis_index("shard")

    def take(row, tile):
        return recv_ref[pl.ds(tile * PAYLOAD + row, SENDERS, stride=SPLIT * PAYLOAD), :]

    for tile in range(SPLIT):
        index_ref[tile * SENDERS:(tile + 1) * SENDERS, :] = take(30, tile).astype(jnp.int32)
    index_ref[SPLIT * SENDERS:(SPLIT + 1) * SENDERS, :] = take(31, 0).astype(jnp.int32)
    copy = pltpu.make_async_copy(index_ref, lists_ref, sem)
    copy.start()

    one = jnp.ones((SENDERS, LANES), jnp.float32)
    nil = jnp.zeros((SENDERS, LANES), jnp.float32)
    order_row = (0, 0, 1, 1, 0, 2)
    order_col = (0, 1, 0, 1, 2, 0)
    pairs = ((0, 0), (0, 1), (0, 2), (1, 1), (1, 2), (2, 2))

    for tile in range(SPLIT):
        half, side = divmod(tile, 2)

        def put(ref, count, first, height, row, value):
            start = (side * count + first + half * SENDERS) * height + row
            ref[pl.ds(start, SENDERS, stride=height), :] = value

        center = [take(a, tile) for a in range(3)]
        norm = (center[0] * center[0] + center[1] * center[1] + center[2] * center[2]) * (-0.5 * LOG2E)
        parts = [split3(c * LOG2E) for c in center]
        norms = split3(norm)
        for k, level in enumerate(order_row):
            for a in range(3):
                put(rowa_ref, ROWS, 0, KPITCH, 3 * k + a, parts[a][level])
        for k in range(3):
            put(rowa_ref, ROWS, 0, KPITCH, 18 + k, norms[k])
            put(rowa_ref, ROWS, 0, KPITCH, 21 + k, one)
        for k in range(24, KEXP):
            put(rowa_ref, ROWS, 0, KPITCH, k, nil)

        for array in range(ARRAYS):
            base = BASES[array]
            first = array * ROWS
            center = [take(base + a, tile) for a in range(3)]
            tangent = [take(base + 3 + a, tile) for a in range(3)]
            norm = (center[0] * center[0] + center[1] * center[1] + center[2] * center[2]) * (-0.5 * LOG2E)
            parts = [split3(c) for c in center]
            norms = split3(norm)
            for k, level in enumerate(order_col):
                for a in range(3):
                    put(colb_ref, COLS + 1, first, KPITCH, 3 * k + a, parts[a][level])
            for k in range(3):
                put(colb_ref, COLS + 1, first, KPITCH, 18 + k, one)
                put(colb_ref, COLS + 1, first, KPITCH, 21 + k, norms[k])
            for k in range(24, KEXP):
                put(colb_ref, COLS + 1, first, KPITCH, k, nil)
            square = tangent[0] * tangent[0] + tangent[1] * tangent[1] + tangent[2] * tangent[2]
            scale = (1.0 if array == 0 else -2.0) / jnp.sqrt(square)
            for n, (a, b) in enumerate(pairs):
                moment = tangent[a] * tangent[b] * scale
                put(colf_ref, COLS + 1, first, FPITCH, n, moment)
                for c in range(3):
                    put(colf_ref, COLS + 1, first, FPITCH, 6 * (c + 1) + n, moment * center[c])

    for side in range(2):
        blank = ((side + 1) * (COLS + 1) - 1)
        colb_ref[blank * KPITCH:blank * KPITCH + KEXP, :] = jnp.zeros((KEXP, LANES), jnp.float32)
        colf_ref[blank * FPITCH:blank * FPITCH + FEATS, :] = jnp.zeros((FEATS, LANES), jnp.float32)
    acc_ref[...] = jnp.zeros(acc_ref.shape, jnp.float32)

    def both(ref, count, block, pitch, height):
        return jnp.concatenate(
            [ref[pl.ds((side * count + block) * pitch, height), :] for side in range(2)], axis=1
        )

    for block in range(ROWS):
        aexp_ref[block] = both(rowa_ref, ROWS, block, KPITCH, KEXP).astype(jnp.bfloat16)

    copy.wait()

    def sender(s, total):
        low = lists_ref[SPLIT * SENDERS + s, me]
        high = lists_ref[SPLIT * SENDERS + s, me + 1]

        def move(k, total):
            flat_ref[total] = lists_ref[lax.shift_right_logical(k, 7) * SENDERS + s, lax.bitwise_and(k, 127)]
            return total + 1

        return lax.fori_loop(low, high, move, total)

    total = lax.fori_loop(0, SENDERS, sender, jnp.int32(0))
    for k in range(UNROLL):
        flat_ref[total + k] = jnp.int32(-1)

    def turn(begin, many):
        for k in range(many):
            code = flat_ref[begin + k]
            dead = code < 0
            r = jnp.where(dead, 0, lax.shift_right_logical(code, 7))
            q = jnp.where(dead, COLS, lax.bitwise_and(code, 127))
            turned = both(colb_ref, COLS + 1, q, KPITCH, KEXP).T.astype(jnp.bfloat16)
            expo = jnp.dot(turned, aexp_ref[r], preferred_element_type=jnp.float32)
            value = jnp.exp2(expo)
            high = value.astype(jnp.bfloat16)
            low = (value - high.astype(jnp.float32)).astype(jnp.bfloat16)
            feats = both(colf_ref, COLS + 1, q, FPITCH, FEATS)
            upper = feats.astype(jnp.bfloat16).astype(jnp.float32)
            feats = jnp.concatenate([upper, feats - upper], axis=0).astype(jnp.bfloat16)
            got = jnp.dot(feats, high, preferred_element_type=jnp.float32)
            got += jnp.dot(feats, low, preferred_element_type=jnp.float32)
            for side in range(2):
                part = pl.ds((side * ROWS + r) * APITCH, 2 * FEATS)
                acc_ref[part, :] += got[:, side * LANES:(side + 1) * LANES]

    turns = lax.div(total + (UNROLL - TAIL - 1), UNROLL)

    @pl.loop(0, turns)
    def _(step):
        turn(step * UNROLL, UNROLL)

    @pl.when(total > turns * UNROLL)
    def _():
        turn(turns * UNROLL, TAIL)

    for tile in range(SPLIT):
        half, side = divmod(tile, 2)
        center = [take(a, tile) for a in range(3)]
        tangent = [take(3 + a, tile) for a in range(3)]

        def moment(f):
            start = (side * ROWS + half * SENDERS) * APITCH + f
            return acc_ref[pl.ds(start, SENDERS, stride=APITCH), :] + acc_ref[
                pl.ds(start + FEATS, SENDERS, stride=APITCH), :
            ]

        square = tangent[0] * tangent[0] + tangent[1] * tangent[1] + tangent[2] * tangent[2]
        inverse = 1.0 / jnp.sqrt(square)
        place = {}
        for n, (a, b) in enumerate(pairs):
            place[a, b] = place[b, a] = n

        def form(offset):
            m = [moment(offset + n) for n in range(6)]
            y = [
                m[place[a, 0]] * tangent[0] + m[place[a, 1]] * tangent[1] + m[place[a, 2]] * tangent[2]
                for a in range(3)
            ]
            return y, (y[0] * tangent[0] + y[1] * tangent[1] + y[2] * tangent[2]) * inverse

        def emit(row, value):
            out_ref[pl.ds(tile * 6 + row, SENDERS, stride=SPLIT * 6), :] = value * (1.0 / B)

        turned, total_k = form(0)
        ratio = total_k / square
        for a in range(3):
            _, pull = form(6 * (a + 1))
            emit(a, pull - center[a] * total_k)
            emit(3 + a, 2.0 * inverse * turned[a] - tangent[a] * ratio)


def per_device(source, target, tile_pairs, tile_counts):
    groups = lax.axis_size("bundle")
    edge = groups // 2
    within = [(g, g ^ 1) for g in range(groups)]
    across = [(2 * z + 1, 2 * z + 2) for z in range(edge - 1)] + [(2 * z + 2, 2 * z + 1) for z in range(edge - 1)]
    far = lax.ppermute(target, "bundle", across)
    near = lax.ppermute(target, "bundle", within)
    vmem = pl.BlockSpec(memory_space=pltpu.VMEM)
    hbm = pl.BlockSpec(memory_space=pltpu.HBM)
    params = pltpu.CompilerParams(vmem_limit_bytes=VMEM_LIMIT)
    slots = tile_pairs.shape[0]
    payload = jax.ShapeDtypeStruct((SENDERS, SPLIT, PAYLOAD, LANES), jnp.float32)
    own = pl.pallas_call(
        own_kernel,
        out_shape=payload,
        in_specs=[pl.BlockSpec(memory_space=pltpu.SMEM), hbm, hbm, hbm],
        out_specs=vmem,
        scratch_shapes=[
            pltpu.VMEM((2, slots), jnp.int32),
            pltpu.VMEM(source.shape, jnp.float32),
            pltpu.VMEM(target.shape, jnp.float32),
            pltpu.VMEM((2, slots), jnp.float32),
            pltpu.SemaphoreType.DMA((3,)),
        ],
        compiler_params=params,
        name="sort_and_pack",
    )(tile_counts, tile_pairs.T, source, target)
    send = pl.pallas_call(
        halo_kernel,
        out_shape=payload,
        in_specs=[vmem] * 3,
        out_specs=vmem,
        input_output_aliases={0: 0},
        compiler_params=params,
        name="pack_neighbours",
    )(own, near, far)
    recv = lax.all_to_all(send, "shard", split_axis=0, concat_axis=0, tiled=True)
    partial = tiles(recv).reshape(SENDERS, SPLIT * 6, LANES)
    back = lax.all_to_all(partial, "shard", split_axis=0, concat_axis=0, tiled=True)
    return pl.pallas_call(
        sum_kernel,
        out_shape=jax.ShapeDtypeStruct((6, 8 * B), jnp.float32),
        in_specs=[vmem],
        out_specs=vmem,
        compiler_params=params,
        name="add_parts",
    )(back)


def sum_kernel(back_ref, out_ref):
    for i in range(SPLIT):
        parts = [back_ref[i * SPLIT + j] for j in range(SPLIT)]
        total = (parts[0] + parts[1]) + (parts[2] + parts[3])
        for tile in range(SPLIT):
            part = pl.ds((i * SPLIT + tile) * LANES, LANES)
            out_ref[:, part] = total[tile * 6:(tile + 1) * 6, :]


def tiles(recv):
    vmem = pl.BlockSpec(memory_space=pltpu.VMEM)
    return pl.pallas_call(
        tile_kernel,
        out_shape=jax.ShapeDtypeStruct((SENDERS * SPLIT * 6, LANES), jnp.float32),
        in_specs=[vmem],
        out_specs=vmem,
        scratch_shapes=[
            pltpu.VMEM(((SPLIT + 1) * SENDERS, LANES), jnp.int32),
            pltpu.SMEM(((SPLIT + 1) * SENDERS, LANES), jnp.int32),
            pltpu.SMEM((SENDERS * 512 + 128,), jnp.int32),
            pltpu.VMEM((2 * (COLS + 1) * KPITCH, LANES), jnp.float32),
            pltpu.VMEM((2 * (COLS + 1) * FPITCH, LANES), jnp.float32),
            pltpu.VMEM((2 * ROWS * KPITCH, LANES), jnp.float32),
            pltpu.VMEM((ROWS, KEXP, B), jnp.bfloat16),
            pltpu.VMEM((2 * ROWS * APITCH, LANES), jnp.float32),
            pltpu.SemaphoreType.DMA,
        ],
        compiler_params=pltpu.CompilerParams(vmem_limit_bytes=VMEM_LIMIT),
        name="tile_gradients",
    )(recv.reshape(SENDERS * SPLIT * PAYLOAD, LANES))


def solution(mesh):
    in_specs = (
        P(None, ("bundle", "shard")),
        P(None, ("bundle", "shard")),
        P(("bundle", "shard"), None),
        P(("bundle", "shard")),
    )
    out_specs = P(None, ("bundle", "shard"))
    return jax.shard_map(
        per_device, mesh=mesh, in_specs=in_specs, out_specs=out_specs, check_vma=False
    )
```

```python
import functools

import jax
import jax.numpy as jnp
from jax import lax
from jax.experimental import pallas as pl
from jax.experimental.pallas import tpu as pltpu
from jax.sharding import PartitionSpec as P

B = 256
LANES = 128
LOG2E = 1.4426950408889634
SENDERS = 16
SPLIT = 4
TARGET_ROWS = 32
OTHER_ROWS = 48
PAYLOAD = TARGET_ROWS + OTHER_ROWS
KEXP = 32
KPITCH = 33
FEATS = 24
FPITCH = 25
APITCH = 49
ROWS = 2 * SENDERS
COLS = 2 * ROWS
UNROLL = 32
TAIL = 16
VMEM_LIMIT = 40 * 1024 * 1024

NT = (((1,), (1,)), ((), ()))
PAIRS = ((0, 0), (0, 1), (0, 2), (1, 1), (1, 2), (2, 2))
PLACE = {(a, b): n for n, pair in enumerate(PAIRS) for a, b in (pair, pair[::-1])}


def shift(value, bits):
    return lax.shift_right_arithmetic(value, bits)


def low_bits(value, mask):
    return lax.bitwise_and(value, mask)


def bucket(row, col):
    taker = SPLIT * low_bits(shift(row, 1), 3) + low_bits(shift(col, 1), 3)
    return 2 * taker + shift(col, 8)


def sort_tiles(count_ref, pairs_ref):
    slots = pairs_ref.shape[1]
    group = lax.axis_index("bundle")
    row = pairs_ref[0:1, :] - group * 128
    col = pairs_ref[1:2, :]
    total_blocks = 8 * 128
    is_source = col < total_blocks
    local = col - jnp.where(is_source, group * 128, total_blocks + (group - 1) * 128)
    step = shift(local, 7)
    step = jnp.where(low_bits(group, 1) == 1, step, 2 - step)
    array = jnp.where(is_source, 0, jnp.where(step == 1, 1, jnp.where(step == 0, 2, 3)))
    local = low_bits(local, 127)
    live = lax.broadcasted_iota(jnp.int32, (1, slots), 1) < count_ref[0]
    key = jnp.where(live, bucket(row, 128 * array + local), 1000)

    lane = lax.broadcasted_iota(jnp.int32, (slots, slots), 1)
    sub = lax.broadcasted_iota(jnp.int32, (slots, slots), 0)
    earlier = (sub < lane).astype(jnp.float32).astype(jnp.bfloat16)
    owner = lax.broadcasted_iota(jnp.int32, (2 * SENDERS, slots), 0)
    mine = (owner == key).astype(jnp.float32)
    rank = jnp.dot(mine.astype(jnp.bfloat16), earlier, preferred_element_type=jnp.float32)
    start = jnp.sum((owner > key).astype(jnp.float32), axis=1, keepdims=True)
    place = jnp.sum(mine * (rank + start), axis=0, keepdims=True).astype(jnp.int32)
    place = jnp.where(live, place, -1)
    onehot = (sub == place).astype(jnp.float32).astype(jnp.bfloat16)
    parts = [part.astype(jnp.float32) for part in (row + 1, array, local)]
    parts = jnp.concatenate(parts + [jnp.zeros((5, slots), jnp.float32)], axis=0)
    moved = lax.dot_general(parts.astype(jnp.bfloat16), onehot, NT, preferred_element_type=jnp.float32)
    return moved[0:1], moved[1:2] * 128.0 + moved[2:3]


def pack_kernel(count_ref, pairs_ref, src_ref, tgt_ref, out_ref):
    row, col = sort_tiles(count_ref, pairs_ref)
    for j in range(SPLIT):
        for tile in range(SPLIT):
            part = pl.ds((j * SPLIT + tile) * LANES, LANES)
            source = src_ref[:, part]
            lanes = slice(tile * LANES, (tile + 1) * LANES)
            first = jnp.concatenate([tgt_ref[:, part], row[:, lanes], col[:, lanes]], axis=0)
            for i in range(SPLIT):
                out_ref[i * SPLIT + j, tile * 8:tile * 8 + 8, :] = first
                base = TARGET_ROWS + tile * 12
                out_ref[j * SPLIT + i, base:base + 6, :] = source
                out_ref[i * SPLIT + j, base + 6:base + 12, :] = source


def split3(value):
    first = value.astype(jnp.bfloat16).astype(jnp.float32)
    rest = value - first
    second = rest.astype(jnp.bfloat16).astype(jnp.float32)
    return first, second, rest - second


def squares(parts):
    return parts[0] * parts[0] + parts[1] * parts[1] + parts[2] * parts[2]


def put(ref, count, first, height, row, tile, value):
    half, side = divmod(tile, 2)
    start = (side * count + first + half * SENDERS) * height + row
    ref[pl.ds(start, SENDERS, stride=height), :] = value


def both(ref, count, block, pitch, height):
    return jnp.concatenate([ref[pl.ds((side * count + block) * pitch, height), :] for side in range(2)], axis=1)


def takers(recv_ref):
    def target(row, tile, ref=recv_ref, height=PAYLOAD):
        return ref[pl.ds(tile * 8 + row, SENDERS, stride=height), :]

    def other(row, tile):
        return recv_ref[pl.ds(TARGET_ROWS + tile * 12 + row, SENDERS, stride=PAYLOAD), :]

    return target, other


def list_tiles(target, codes_ref, lists_ref, sem, which):
    me = lax.axis_index("shard")
    before = jnp.zeros((SENDERS, LANES), jnp.float32)
    many = before
    for tile in range(SPLIT):
        row = target(6, tile).astype(jnp.int32) - 1
        col = target(7, tile).astype(jnp.int32)
        key = jnp.where(row < 0, 1000, bucket(row, col))
        before += (key < 2 * me + which).astype(jnp.float32)
        many += (key == 2 * me + which).astype(jnp.float32)
        rindex = low_bits(shift(row, 3), 15) + SENDERS * low_bits(row, 1)
        cindex = ROWS * low_bits(shift(col, 7), 1) + low_bits(shift(col, 3), 15) + SENDERS * low_bits(col, 1)
        codes_ref[tile * SENDERS:(tile + 1) * SENDERS, :] = rindex * 128 + cindex
    lane = lax.broadcasted_iota(jnp.int32, (SENDERS, LANES), 1)
    before = jnp.sum(before, axis=1, keepdims=True)
    many = jnp.sum(many, axis=1, keepdims=True)
    codes_ref[SPLIT * SENDERS:(SPLIT + 1) * SENDERS, :] = jnp.where(lane == 0, before, many).astype(jnp.int32)
    copy = pltpu.make_async_copy(codes_ref, lists_ref, sem)
    copy.start()
    return copy


def flatten(lists_ref, flat_ref):
    def sender(s, total):
        low = lists_ref[SPLIT * SENDERS + s, 0]
        count = lists_ref[SPLIT * SENDERS + s, 1]

        def move(step, carry):
            for u in range(8):
                k = low + step * 8 + u
                flat_ref[total + step * 8 + u] = lists_ref[shift(k, 7) * SENDERS + s, low_bits(k, 127)]
            return carry

        lax.fori_loop(0, shift(count + 7, 3), move, 0)
        return total + count

    total = lax.fori_loop(0, SENDERS, sender, jnp.int32(0))
    for k in range(UNROLL):
        flat_ref[total + k] = jnp.int32(-1)
    return total


def row_operand(other, rowa_ref, aexp_ref):
    nil = jnp.zeros((SENDERS, LANES), jnp.float32)
    for tile in range(SPLIT):
        center = [other(a, tile) for a in range(3)]
        parts = [split3(c * LOG2E) for c in center]
        norms = split3(squares(center) * (-0.5 * LOG2E))
        for k, level in enumerate((0, 0, 1, 1, 0, 2)):
            for a in range(3):
                put(rowa_ref, ROWS, 0, KPITCH, 3 * k + a, tile, parts[a][level])
        for k in range(3):
            put(rowa_ref, ROWS, 0, KPITCH, 18 + k, tile, norms[k])
            put(rowa_ref, ROWS, 0, KPITCH, 21 + k, tile, nil + 1.0)
        for k in range(24, KEXP):
            put(rowa_ref, ROWS, 0, KPITCH, k, tile, nil)
    for block in range(ROWS):
        aexp_ref[block] = both(rowa_ref, ROWS, block, KPITCH, KEXP).astype(jnp.bfloat16)


def column_operands(columns, weights, colb_ref, colf_ref):
    nil = jnp.zeros((SENDERS, LANES), jnp.float32)
    for array, (read, weight) in enumerate(zip(columns, weights)):
        first = array * ROWS
        for tile in range(SPLIT):
            center = [read(a, tile) for a in range(3)]
            tangent = [read(3 + a, tile) for a in range(3)]
            parts = [split3(c) for c in center]
            norms = split3(squares(center) * (-0.5 * LOG2E))
            for k, level in enumerate((0, 1, 0, 1, 2, 0)):
                for a in range(3):
                    put(colb_ref, COLS + 1, first, KPITCH, 3 * k + a, tile, parts[a][level])
            for k in range(3):
                put(colb_ref, COLS + 1, first, KPITCH, 18 + k, tile, nil + 1.0)
                put(colb_ref, COLS + 1, first, KPITCH, 21 + k, tile, norms[k])
            for k in range(24, KEXP):
                put(colb_ref, COLS + 1, first, KPITCH, k, tile, nil)
            scale = weight / jnp.sqrt(squares(tangent))
            for n, (a, b) in enumerate(PAIRS):
                moment = tangent[a] * tangent[b] * scale
                put(colf_ref, COLS + 1, first, FPITCH, n, tile, moment)
                for c in range(3):
                    put(colf_ref, COLS + 1, first, FPITCH, 6 * (c + 1) + n, tile, moment * center[c])
    for side in range(2):
        blank = (side + 1) * (COLS + 1) - 1
        colb_ref[blank * KPITCH:blank * KPITCH + KEXP, :] = jnp.zeros((KEXP, LANES), jnp.float32)
        colf_ref[blank * FPITCH:blank * FPITCH + FEATS, :] = jnp.zeros((FEATS, LANES), jnp.float32)


def add_tiles(total, flat_ref, colb_ref, colf_ref, aexp_ref, acc_ref):
    def turn(begin, many):
        for k in range(many):
            code = flat_ref[begin + k]
            dead = code < 0
            r = jnp.where(dead, 0, lax.shift_right_logical(code, 7))
            q = jnp.where(dead, COLS, low_bits(code, 127))
            turned = both(colb_ref, COLS + 1, q, KPITCH, KEXP).T.astype(jnp.bfloat16)
            expo = jnp.dot(turned, aexp_ref[r], preferred_element_type=jnp.float32)
            value = jnp.exp2(expo)
            high = value.astype(jnp.bfloat16)
            low = (value - high.astype(jnp.float32)).astype(jnp.bfloat16)
            feats = both(colf_ref, COLS + 1, q, FPITCH, FEATS)
            upper = feats.astype(jnp.bfloat16).astype(jnp.float32)
            feats = jnp.concatenate([upper, feats - upper], axis=0).astype(jnp.bfloat16)
            got = jnp.dot(feats, high, preferred_element_type=jnp.float32)
            extra = jnp.dot(feats[0:32], low, preferred_element_type=jnp.float32)
            got = jnp.concatenate([got[0:FEATS] + extra[0:FEATS], got[FEATS:]], axis=0)
            for side in range(2):
                part = pl.ds((side * ROWS + r) * APITCH, 2 * FEATS)
                acc_ref[part, :] += got[:, side * LANES:(side + 1) * LANES]

    turns = lax.div(total + (UNROLL - TAIL - 1), UNROLL)

    @pl.loop(0, turns)
    def _(step):
        turn(step * UNROLL, UNROLL)

    @pl.when(total > turns * UNROLL)
    def _():
        turn(turns * UNROLL, TAIL)


def own_kernel(recv_ref, acc_ref, codes_ref, lists_ref, flat_ref, colb_ref, colf_ref, rowa_ref, aexp_ref, sem):
    target, other = takers(recv_ref)
    copy = list_tiles(target, codes_ref, lists_ref, sem, 0)
    row_operand(other, rowa_ref, aexp_ref)
    column_operands((lambda row, tile: other(6 + row, tile), target), (1.0, -2.0), colb_ref, colf_ref)
    acc_ref[...] = jnp.zeros(acc_ref.shape, jnp.float32)
    copy.wait()
    add_tiles(flatten(lists_ref, flat_ref), flat_ref, colb_ref, colf_ref, aexp_ref, acc_ref)


def last_kernel(
    recv_ref, near_ref, far_ref, own_ref, out_ref, acc_ref, codes_ref, lists_ref, flat_ref, colb_ref, colf_ref, rowa_ref,
    aexp_ref, sem,
):
    target, other = takers(recv_ref)
    copy = list_tiles(target, codes_ref, lists_ref, sem, 1)
    row_operand(other, rowa_ref, aexp_ref)
    readers = [functools.partial(target, ref=ref, height=TARGET_ROWS) for ref in (near_ref, far_ref)]
    column_operands(readers, (-2.0, -2.0), colb_ref, colf_ref)
    acc_ref[...] = own_ref[...]
    copy.wait()
    add_tiles(flatten(lists_ref, flat_ref), flat_ref, colb_ref, colf_ref, aexp_ref, acc_ref)

    for tile in range(SPLIT):
        half, side = divmod(tile, 2)
        center = [other(a, tile) for a in range(3)]
        tangent = [other(3 + a, tile) for a in range(3)]

        def moment(f):
            start = (side * ROWS + half * SENDERS) * APITCH + f
            high = acc_ref[pl.ds(start, SENDERS, stride=APITCH), :]
            return high + acc_ref[pl.ds(start + FEATS, SENDERS, stride=APITCH), :]

        square = squares(tangent)
        inverse = 1.0 / jnp.sqrt(square)

        def form(offset):
            m = [moment(offset + n) for n in range(6)]
            y = [sum(m[PLACE[a, b]] * tangent[b] for b in range(3)) for a in range(3)]
            return y, (y[0] * tangent[0] + y[1] * tangent[1] + y[2] * tangent[2]) * inverse

        def emit(row, value):
            out_ref[pl.ds(tile * 6 + row, SENDERS, stride=SPLIT * 6), :] = value * (1.0 / B)

        turned, total_k = form(0)
        ratio = total_k / square
        for a in range(3):
            _, pull = form(6 * (a + 1))
            emit(a, pull - center[a] * total_k)
            emit(3 + a, 2.0 * inverse * turned[a] - tangent[a] * ratio)


def sum_kernel(back_ref, out_ref):
    for i in range(SPLIT):
        parts = [back_ref[i * SPLIT + j] for j in range(SPLIT)]
        total = (parts[0] + parts[1]) + (parts[2] + parts[3])
        for tile in range(SPLIT):
            part = pl.ds((i * SPLIT + tile) * LANES, LANES)
            out_ref[:, part] = total[tile * 6:(tile + 1) * 6, :]


def tile_scratch():
    return [
        pltpu.VMEM(((SPLIT + 1) * SENDERS, LANES), jnp.int32),
        pltpu.SMEM(((SPLIT + 1) * SENDERS, LANES), jnp.int32),
        pltpu.SMEM((SENDERS * 512 + 128,), jnp.int32),
        pltpu.VMEM((2 * (COLS + 1) * KPITCH, LANES), jnp.float32),
        pltpu.VMEM((2 * (COLS + 1) * FPITCH, LANES), jnp.float32),
        pltpu.VMEM((2 * ROWS * KPITCH, LANES), jnp.float32),
        pltpu.VMEM((ROWS, KEXP, B), jnp.bfloat16),
    ]


def call(kernel, name, out, inputs, scratch=(), smem=0, flops=0):
    vmem = pl.BlockSpec(memory_space=pltpu.VMEM)
    return pl.pallas_call(
        kernel,
        out_shape=jax.ShapeDtypeStruct(out, jnp.float32),
        in_specs=[pl.BlockSpec(memory_space=pltpu.SMEM)] * smem + [vmem] * (len(inputs) - smem),
        out_specs=vmem,
        scratch_shapes=list(scratch),
        compiler_params=pltpu.CompilerParams(vmem_limit_bytes=VMEM_LIMIT),
        cost_estimate=pl.CostEstimate(flops=flops, bytes_accessed=1 << 20, transcendentals=0) if flops else None,
        name=name,
    )(*inputs)


def own_tiles(recv):
    acc = (2 * ROWS * APITCH, LANES)
    return call(own_kernel, "own_tiles", acc, (recv,), tile_scratch() + [pltpu.SemaphoreType.DMA], flops=10**10)


def last_tiles(recv, near, far, acc):
    scratch = [pltpu.VMEM(acc.shape, jnp.float32)] + tile_scratch() + [pltpu.SemaphoreType.DMA]
    out = (SENDERS * SPLIT * 6, LANES)
    return call(last_kernel, "last_tiles", out, (recv, near, far, acc), scratch, flops=10**9)


def per_device(source, target, tile_pairs, tile_counts):
    groups = lax.axis_size("bundle")
    chips = groups // 2
    within = [(g, g ^ 1) for g in range(groups)]
    across = [(2 * z + 1, 2 * z + 2) for z in range(chips - 1)] + [(2 * z + 2, 2 * z + 1) for z in range(chips - 1)]
    send = call(
        pack_kernel, "sort_and_pack", (SENDERS, PAYLOAD, LANES), (tile_counts, tile_pairs.T, source, target), smem=1
    )
    recv = lax.all_to_all(send, "shard", split_axis=0, concat_axis=0, tiled=True)
    shared = recv[:, 0:TARGET_ROWS]
    far = lax.ppermute(shared, "bundle", across).reshape(SENDERS * TARGET_ROWS, LANES)
    near = lax.ppermute(shared, "bundle", within).reshape(SENDERS * TARGET_ROWS, LANES)
    recv = recv.reshape(SENDERS * PAYLOAD, LANES)
    partial = last_tiles(recv, near, far, own_tiles(recv)).reshape(SENDERS, SPLIT * 6, LANES)
    back = lax.all_to_all(partial, "shard", split_axis=0, concat_axis=0, tiled=True)
    return call(sum_kernel, "add_parts", (6, 8 * B), (back,))


def solution(mesh):
    in_specs = (
        P(None, ("bundle", "shard")),
        P(None, ("bundle", "shard")),
        P(("bundle", "shard"), None),
        P(("bundle", "shard")),
    )
    out_specs = P(None, ("bundle", "shard"))
    return jax.shard_map(
        per_device, mesh=mesh, in_specs=in_specs, out_specs=out_specs, check_vma=False
    )
```

```python
import jax
import jax.numpy as jnp
from jax import lax
from jax.experimental import pallas as pl
from jax.experimental.pallas import tpu as pltpu
from jax.sharding import PartitionSpec as P

B = 256
LANES = 128
LOG2E = 1.4426950408889634
SIDE = 4
BLOCKS = 8
PART = 6 * 2 * BLOCKS
LISTS = 8
PAYLOAD = 2 * PART + LISTS
ACROSS = PART + SIDE * LISTS
KEXP = 32
KPITCH = 33
FEATS = 24
FPITCH = 25
APITCH = 49
ROWS = SIDE * BLOCKS
COLS = 4 * ROWS
UNROLL = 32
TAILS = (16, 8)
VMEM_LIMIT = 40 * 1024 * 1024
PACK_LIMIT = 60 * 1024 * 1024

NT = (((1,), (1,)), ((), ()))
PAIRS = ((0, 0), (0, 1), (0, 2), (1, 1), (1, 2), (2, 2))
PLACE = {(a, b): n for n, pair in enumerate(PAIRS) for a, b in (pair, pair[::-1])}


def shift(value, bits):
    return lax.shift_right_arithmetic(value, bits)


def low_bits(value, mask):
    return lax.bitwise_and(value, mask)


def taker(row, col):
    return SIDE * shift(row, 5) + low_bits(shift(col, 3), 3)


def sort_tiles(count_ref, pairs_ref):
    slots = pairs_ref.shape[1]
    group = lax.axis_index("bundle")
    row = pairs_ref[0:1, :] - group * 128
    col = pairs_ref[1:2, :]
    total_blocks = 8 * 128
    is_source = col < total_blocks
    local = col - jnp.where(is_source, group * 128, total_blocks + (group - 1) * 128)
    step = shift(local, 7)
    step = jnp.where(low_bits(group, 1) == 1, step, 2 - step)
    array = jnp.where(is_source, 0, jnp.where(step == 1, 1, jnp.where(step == 0, 2, 3)))
    local = low_bits(local, 127)
    live = lax.broadcasted_iota(jnp.int32, (1, slots), 1) < count_ref[0]
    key = jnp.where(live, taker(row, local), 1000)

    lane = lax.broadcasted_iota(jnp.int32, (slots, slots), 1)
    sub = lax.broadcasted_iota(jnp.int32, (slots, slots), 0)
    earlier = (sub < lane).astype(jnp.float32).astype(jnp.bfloat16)
    owner = lax.broadcasted_iota(jnp.int32, (SIDE * SIDE, slots), 0)
    mine = (owner == key).astype(jnp.float32)
    rank = jnp.dot(mine.astype(jnp.bfloat16), earlier, preferred_element_type=jnp.float32)
    start = jnp.sum((owner > key).astype(jnp.float32), axis=1, keepdims=True)
    place = jnp.sum(mine * (rank + start), axis=0, keepdims=True).astype(jnp.int32)
    place = jnp.where(live, place, -1)
    onehot = (sub == place).astype(jnp.float32).astype(jnp.bfloat16)
    parts = [part.astype(jnp.float32) for part in (row + 1, array, local)]
    parts = jnp.concatenate(parts + [jnp.zeros((5, slots), jnp.float32)], axis=0)
    moved = lax.dot_general(parts.astype(jnp.bfloat16), onehot, NT, preferred_element_type=jnp.float32)
    return moved[0:1], moved[1:2] * 128.0 + moved[2:3]


def pack_kernel(count_in, pairs_in, src_in, tgt_in, out_ref, count_ref, pairs_ref, src_ref, tgt_ref, sems):
    moves = ((count_in, count_ref), (pairs_in, pairs_ref), (src_in, src_ref), (tgt_in, tgt_ref))
    copies = [pltpu.make_async_copy(given, taken, sems.at[n]) for n, (given, taken) in enumerate(moves)]
    for copy in copies:
        copy.start()
    copies[0].wait()
    copies[1].wait()
    lists = sort_tiles(count_ref, pairs_ref)
    for n, numbers in enumerate(lists):
        for tile in range(SIDE):
            at = 2 * PART + SIDE * n + tile
            out_ref[at:at + 1, :] = numbers[:, tile * LANES:(tile + 1) * LANES]
    for n, ref in enumerate((tgt_ref, src_ref)):
        copies[3 - n].wait()
        for block in range(BLOCKS):
            for side in range(2):
                lanes = pl.ds((2 * block + side) * LANES, LANES)
                out_ref[pl.ds(n * PART + side * BLOCKS + block, 6, stride=2 * BLOCKS), :] = ref[:, lanes]
    for peer in range(1, SIDE):
        out_ref[peer * PAYLOAD:(peer + 1) * PAYLOAD, :] = out_ref[0:PAYLOAD, :]


def split3(value):
    first = value.astype(jnp.bfloat16).astype(jnp.float32)
    rest = value - first
    second = rest.astype(jnp.bfloat16).astype(jnp.float32)
    return first, second, rest - second


def squares(parts):
    return parts[0] * parts[0] + parts[1] * parts[1] + parts[2] * parts[2]


def put(ref, count, first, height, row, value):
    for side in range(2):
        start = (side * count + first) * height + row
        ref[pl.ds(start, BLOCKS, stride=height), :] = value[side * BLOCKS:(side + 1) * BLOCKS]


def component(ref, base, row):
    return ref[base + row * 2 * BLOCKS:base + (row + 1) * 2 * BLOCKS, :]


def both(ref, count, block, pitch, height):
    return jnp.concatenate([ref[pl.ds((side * count + block) * pitch, height), :] for side in range(2)], axis=1)


def list_tiles(across, codes_ref):
    me = lax.axis_index("shard")
    here = low_bits(me, 3)
    size = SIDE * SIDE
    sub = lax.broadcasted_iota(jnp.int32, (size, size), 0)
    along = lax.broadcasted_iota(jnp.int32, (size, size), 1)
    same = (shift(sub, 2) == shift(along, 2)).astype(jnp.float32).astype(jnp.bfloat16)
    lane = lax.broadcasted_iota(jnp.int32, (size, LANES), 1)
    for p, ref in enumerate(across):
        row = ref[PART:PART + size, :].astype(jnp.int32) - 1
        col = ref[PART + size:PART + 2 * size, :].astype(jnp.int32)
        local = low_bits(col, 127)
        key = jnp.where(row < 0, 1000, taker(row, local))
        rindex = BLOCKS * low_bits(here - shift(row, 3), 3) + low_bits(row, 7)
        cindex = ROWS * shift(col, 7) + BLOCKS * shift(local, 5) + low_bits(local, 7)
        codes_ref[p * size:(p + 1) * size, :] = rindex * 128 + cindex
        before = jnp.sum((key < me).astype(jnp.float32), axis=1, keepdims=True)
        many = jnp.sum((key == me).astype(jnp.float32), axis=1, keepdims=True)
        both_counts = jnp.where(lane == 0, before, many).astype(jnp.bfloat16)
        both_counts = jnp.dot(same, both_counts, preferred_element_type=jnp.float32)
        codes_ref[(SIDE + p) * size:(SIDE + p + 1) * size, :] = both_counts.astype(jnp.int32)


def flatten(lists_ref, flat_ref):
    def sender(s, total):
        low = lists_ref[SIDE * (SIDE * SIDE + s), 0]
        count = lists_ref[SIDE * (SIDE * SIDE + s), 1]

        def move(step, carry):
            for u in range(8):
                k = low + step * 8 + u
                flat_ref[total + step * 8 + u] = lists_ref[SIDE * s + shift(k, 7), low_bits(k, 127)]
            return carry

        lax.fori_loop(0, shift(count + 7, 3), move, 0)
        return total + count

    total = lax.fori_loop(0, SIDE * SIDE, sender, jnp.int32(0))
    for k in range(UNROLL):
        flat_ref[total + k] = jnp.int32(-1)
    return total


def row_operand(across, rowa_ref, aexp_ref):
    nil = jnp.zeros((2 * BLOCKS, LANES), jnp.float32)
    for p, ref in enumerate(across):
        center = [component(ref, 0, a) for a in range(3)]
        parts = [split3(c * LOG2E) for c in center]
        norms = split3(squares(center) * (-0.5 * LOG2E))
        first = p * BLOCKS
        for k, level in enumerate((0, 0, 1, 1, 0, 2)):
            for a in range(3):
                put(rowa_ref, ROWS, first, KPITCH, 3 * k + a, parts[a][level])
        for k in range(3):
            put(rowa_ref, ROWS, first, KPITCH, 18 + k, norms[k])
            put(rowa_ref, ROWS, first, KPITCH, 21 + k, nil + 1.0)
        for k in range(24, KEXP):
            put(rowa_ref, ROWS, first, KPITCH, k, nil)
    for block in range(ROWS):
        aexp_ref[block] = both(rowa_ref, ROWS, block, KPITCH, KEXP).astype(jnp.bfloat16)


def column_operands(columns, weights, colb_ref, colf_ref):
    nil = jnp.zeros((2 * BLOCKS, LANES), jnp.float32)
    for array, ((ref, base, height), weight) in enumerate(zip(columns, weights)):
        for x in range(SIDE):
            first = array * ROWS + x * BLOCKS
            center = [component(ref, base + x * height, a) for a in range(3)]
            tangent = [component(ref, base + x * height, 3 + a) for a in range(3)]
            parts = [split3(c) for c in center]
            norms = split3(squares(center) * (-0.5 * LOG2E))
            for k, level in enumerate((0, 1, 0, 1, 2, 0)):
                for a in range(3):
                    put(colb_ref, COLS + 1, first, KPITCH, 3 * k + a, parts[a][level])
            for k in range(3):
                put(colb_ref, COLS + 1, first, KPITCH, 18 + k, nil + 1.0)
                put(colb_ref, COLS + 1, first, KPITCH, 21 + k, norms[k])
            for k in range(24, KEXP):
                put(colb_ref, COLS + 1, first, KPITCH, k, nil)
            scale = weight / jnp.sqrt(squares(tangent))
            for n, (a, b) in enumerate(PAIRS):
                moment = tangent[a] * tangent[b] * scale
                put(colf_ref, COLS + 1, first, FPITCH, n, moment)
                for c in range(3):
                    put(colf_ref, COLS + 1, first, FPITCH, 6 * (c + 1) + n, moment * center[c])
    for side in range(2):
        blank = (side + 1) * (COLS + 1) - 1
        colb_ref[blank * KPITCH:blank * KPITCH + KEXP, :] = jnp.zeros((KEXP, LANES), jnp.float32)
        colf_ref[blank * FPITCH:blank * FPITCH + FEATS, :] = jnp.zeros((FEATS, LANES), jnp.float32)


def add_tiles(total, flat_ref, colb_ref, colf_ref, aexp_ref, acc_ref):
    def turn(begin, many):
        for k in range(many):
            code = flat_ref[begin + k]
            dead = code < 0
            r = jnp.where(dead, 0, lax.shift_right_logical(code, 7))
            q = jnp.where(dead, COLS, low_bits(code, 127))
            turned = both(colb_ref, COLS + 1, q, KPITCH, KEXP).T.astype(jnp.bfloat16)
            expo = jnp.dot(turned, aexp_ref[r], preferred_element_type=jnp.float32)
            value = jnp.exp2(expo)
            high = value.astype(jnp.bfloat16)
            low = (value - high.astype(jnp.float32)).astype(jnp.bfloat16)
            feats = both(colf_ref, COLS + 1, q, FPITCH, FEATS)
            upper = feats.astype(jnp.bfloat16).astype(jnp.float32)
            feats = jnp.concatenate([upper, feats - upper], axis=0).astype(jnp.bfloat16)
            got = jnp.dot(feats, high, preferred_element_type=jnp.float32)
            extra = jnp.dot(feats[0:32], low, preferred_element_type=jnp.float32)
            got = jnp.concatenate([got[0:FEATS] + extra[0:FEATS], got[FEATS:]], axis=0)
            for side in range(2):
                part = pl.ds((side * ROWS + r) * APITCH, 2 * FEATS)
                acc_ref[part, :] += got[:, side * LANES:(side + 1) * LANES]

    turns = lax.div(total + (UNROLL - sum(TAILS) - 1), UNROLL)
    rest = total - turns * UNROLL

    @pl.loop(0, turns)
    def _(step):
        turn(step * UNROLL, UNROLL)

    @pl.when(rest > TAILS[1])
    def _():
        turn(turns * UNROLL, TAILS[0])

    @pl.when((rest > 0) & (low_bits(rest - 1, TAILS[1]) == 0))
    def _():
        turn(turns * UNROLL + jnp.where(rest > TAILS[1], TAILS[0], 0), TAILS[1])


def split_kernel(recv_ref, shared_ref, across_ref):
    x = shift(lax.axis_index("shard"), 2)
    for peer in range(SIDE):
        base = peer * PAYLOAD
        shared_ref[peer * PART:(peer + 1) * PART, :] = recv_ref[base:base + PART, :]
        for n in range(2):
            to = PART + SIDE * (SIDE * n + peer)
            across_ref[to:to + SIDE, :] = recv_ref[base + 2 * PART + SIDE * n:base + 2 * PART + SIDE * (n + 1), :]
    across_ref[0:PART, :] = recv_ref[pl.ds(pl.multiple_of(x * PAYLOAD + PART, 8), PART), :]


def tile_kernel(
    recv_ref, near_ref, far_ref, across0, across1, across2, across3, out0, out1, out2, out3, codes_ref, colb_ref,
    colf_ref, rowa_ref, aexp_ref, acc_ref, lists_ref, flat_ref, sem,
):
    across = (across0, across1, across2, across3)
    list_tiles(across, codes_ref)
    copy = pltpu.make_async_copy(codes_ref, lists_ref, sem)
    copy.start()
    row_operand(across, rowa_ref, aexp_ref)
    columns = ((recv_ref, PART, PAYLOAD), (recv_ref, 0, PAYLOAD), (near_ref, 0, PART), (far_ref, 0, PART))
    column_operands(columns, (1.0, -2.0, -2.0, -2.0), colb_ref, colf_ref)
    acc_ref[...] = jnp.zeros(acc_ref.shape, jnp.float32)
    copy.wait()
    add_tiles(flatten(lists_ref, flat_ref), flat_ref, colb_ref, colf_ref, aexp_ref, acc_ref)

    for p, (ref, out_ref) in enumerate(zip(across, (out0, out1, out2, out3))):
        center = [component(ref, 0, a) for a in range(3)]
        tangent = [component(ref, 0, 3 + a) for a in range(3)]

        def moment(f):
            halves = []
            for side in range(2):
                start = (side * ROWS + p * BLOCKS) * APITCH + f
                high = acc_ref[pl.ds(start, BLOCKS, stride=APITCH), :]
                halves.append(high + acc_ref[pl.ds(start + FEATS, BLOCKS, stride=APITCH), :])
            return jnp.concatenate(halves, axis=0)

        square = squares(tangent)
        inverse = 1.0 / jnp.sqrt(square)

        def form(offset):
            m = [moment(offset + n) for n in range(6)]
            y = [sum(m[PLACE[a, b]] * tangent[b] for b in range(3)) for a in range(3)]
            return y, (y[0] * tangent[0] + y[1] * tangent[1] + y[2] * tangent[2]) * inverse

        def emit(row, value):
            out_ref[row * 2 * BLOCKS:(row + 1) * 2 * BLOCKS, :] = value * (1.0 / B)

        turned, total_k = form(0)
        ratio = total_k / square
        for a in range(3):
            _, pull = form(6 * (a + 1))
            emit(a, pull - center[a] * total_k)
            emit(3 + a, 2.0 * inverse * turned[a] - tangent[a] * ratio)


def sum_kernel(part0, part1, part2, part3, out_ref, total_ref):
    total_ref[...] = (part0[...] + part1[...]) + (part2[...] + part3[...])
    for block in range(BLOCKS):
        for side in range(2):
            lanes = pl.ds((2 * block + side) * LANES, LANES)
            out_ref[:, lanes] = total_ref[pl.ds(side * BLOCKS + block, 6, stride=2 * BLOCKS), :]


CODES = (2 * SIDE * SIDE * SIDE, LANES)
ACC = (2 * ROWS * APITCH, LANES)
COLB = (2 * (COLS + 1) * KPITCH, LANES)
COLF = (2 * (COLS + 1) * FPITCH, LANES)


def array(shape, dtype=jnp.float32):
    return jax.ShapeDtypeStruct(shape, dtype)


def call(kernel, name, out, inputs, scratch=(), flops=0, hbm=False, limit=VMEM_LIMIT):
    vmem = pl.BlockSpec(memory_space=pltpu.VMEM)
    given = pl.BlockSpec(memory_space=pl.ANY) if hbm else vmem
    return pl.pallas_call(
        kernel,
        out_shape=out,
        in_specs=[given] * len(inputs),
        out_specs=jax.tree.map(lambda _: vmem, out),
        scratch_shapes=list(scratch),
        compiler_params=pltpu.CompilerParams(vmem_limit_bytes=limit),
        cost_estimate=pl.CostEstimate(flops=flops, bytes_accessed=1 << 20, transcendentals=0) if flops else None,
        name=name,
    )(*inputs)


def tiles(recv, near, far, across):
    scratch = [
        pltpu.VMEM(CODES, jnp.int32),
        pltpu.VMEM(COLB, jnp.float32),
        pltpu.VMEM(COLF, jnp.float32),
        pltpu.VMEM((2 * ROWS * KPITCH, LANES), jnp.float32),
        pltpu.VMEM((ROWS, KEXP, B), jnp.bfloat16),
        pltpu.VMEM(ACC, jnp.float32),
        pltpu.SMEM(CODES, jnp.int32),
        pltpu.SMEM((SIDE * SIDE * 512 + 128,), jnp.int32),
        pltpu.SemaphoreType.DMA,
    ]
    out = (array((PART, LANES)),) * SIDE
    return call(tile_kernel, "tile_gradients", out, (recv, near, far, *across), scratch, flops=10**10)


def per_device(source, target, tile_pairs, tile_counts):
    groups = lax.axis_size("bundle")
    chips = groups // 2
    within = [(g, g ^ 1) for g in range(groups)]
    between = [(2 * z + 1, 2 * z + 2) for z in range(chips - 1)] + [(2 * z + 2, 2 * z + 1) for z in range(chips - 1)]

    def along_y(step):
        return [(SIDE * x + y, SIDE * x + (y + step) % SIDE) for x in range(SIDE) for y in range(SIDE)]

    slots = tile_pairs.shape[0]
    scratch = [
        pltpu.SMEM(tile_counts.shape, jnp.int32),
        pltpu.VMEM((2, slots), jnp.int32),
        pltpu.VMEM(source.shape, jnp.float32),
        pltpu.VMEM(target.shape, jnp.float32),
        pltpu.SemaphoreType.DMA((4,)),
    ]
    send = call(
        pack_kernel, "sort_and_pack", array((SIDE * PAYLOAD, LANES)), (tile_counts, tile_pairs.T, source, target),
        scratch, hbm=True, limit=PACK_LIMIT,
    )
    rings = [[SIDE * x + y for x in range(SIDE)] for y in range(SIDE)]
    recv = lax.all_to_all(send, "shard", split_axis=0, concat_axis=0, tiled=True, axis_index_groups=rings)
    shared, across = call(
        split_kernel, "split", (array((SIDE * PART, LANES)), array((ACROSS, LANES))), (recv,)
    )
    near = lax.ppermute(shared, "bundle", within)
    far = lax.ppermute(shared, "bundle", between)
    passed = [lax.ppermute(across, "shard", along_y(step)) for step in range(1, SIDE)]
    parts = tiles(recv, near, far, (across, *passed))
    back = [lax.ppermute(parts[step], "shard", along_y(-step)) for step in range(1, SIDE)]
    return call(
        sum_kernel, "add_parts", array((6, 8 * B)), (parts[0], *back), [pltpu.VMEM((PART, LANES), jnp.float32)]
    )


def solution(mesh):
    in_specs = (
        P(None, ("bundle", "shard")),
        P(None, ("bundle", "shard")),
        P(("bundle", "shard"), None),
        P(("bundle", "shard")),
    )
    out_specs = P(None, ("bundle", "shard"))
    return jax.shard_map(
        per_device, mesh=mesh, in_specs=in_specs, out_specs=out_specs, check_vma=False
    )
```

```python
import jax
import jax.numpy as jnp
from jax import lax
from jax.experimental import pallas as pl
from jax.experimental.pallas import tpu as pltpu
from jax.sharding import PartitionSpec as P

B = 256
LANES = 128
LOG2E = 1.4426950408889634
SIDE = 4
BLOCKS = 8
PART = 6 * 2 * BLOCKS
LISTS = 8
PAYLOAD = 2 * PART + LISTS
ACROSS = PART + SIDE * LISTS
KEXP = 32
KPITCH = 33
FEATS = 24
FPITCH = 25
APITCH = 49
ROWS = SIDE * BLOCKS
COLS = 4 * ROWS
UNROLL = 32
TAILS = (16, 8)
VMEM_LIMIT = 40 * 1024 * 1024
PACK_LIMIT = 60 * 1024 * 1024

NT = (((1,), (1,)), ((), ()))
PAIRS = ((0, 0), (0, 1), (0, 2), (1, 1), (1, 2), (2, 2))
PLACE = {(a, b): n for n, pair in enumerate(PAIRS) for a, b in (pair, pair[::-1])}


def shift(value, bits):
    return lax.shift_right_arithmetic(value, bits)


def low_bits(value, mask):
    return lax.bitwise_and(value, mask)


def taker(row, col):
    return SIDE * shift(row, 5) + low_bits(shift(col, 3), 3)


def sort_tiles(count_ref, pairs_ref):
    slots = pairs_ref.shape[1]
    group = lax.axis_index("bundle")
    row = pairs_ref[0:1, :] - group * 128
    col = pairs_ref[1:2, :]
    total_blocks = 8 * 128
    is_source = col < total_blocks
    local = col - jnp.where(is_source, group * 128, total_blocks + (group - 1) * 128)
    step = shift(local, 7)
    step = jnp.where(low_bits(group, 1) == 1, step, 2 - step)
    array = jnp.where(is_source, 0, jnp.where(step == 1, 1, jnp.where(step == 0, 2, 3)))
    local = low_bits(local, 127)
    live = lax.broadcasted_iota(jnp.int32, (1, slots), 1) < count_ref[0]
    key = jnp.where(live, taker(row, local), 1000)

    lane = lax.broadcasted_iota(jnp.int32, (slots, slots), 1)
    sub = lax.broadcasted_iota(jnp.int32, (slots, slots), 0)
    earlier = (sub < lane).astype(jnp.float32).astype(jnp.bfloat16)
    owner = lax.broadcasted_iota(jnp.int32, (SIDE * SIDE, slots), 0)
    mine = (owner == key).astype(jnp.float32)
    rank = jnp.dot(mine.astype(jnp.bfloat16), earlier, preferred_element_type=jnp.float32)
    start = jnp.sum((owner > key).astype(jnp.float32), axis=1, keepdims=True)
    place = jnp.sum(mine * (rank + start), axis=0, keepdims=True).astype(jnp.int32)
    place = jnp.where(live, place, -1)
    onehot = (sub == place).astype(jnp.float32).astype(jnp.bfloat16)
    parts = [part.astype(jnp.float32) for part in (row + 1, array, local)]
    parts = jnp.concatenate(parts + [jnp.zeros((5, slots), jnp.float32)], axis=0)
    moved = lax.dot_general(parts.astype(jnp.bfloat16), onehot, NT, preferred_element_type=jnp.float32)
    return moved[0:1], moved[1:2] * 128.0 + moved[2:3]


def pack_kernel(count_in, pairs_in, src_in, tgt_in, out_ref, count_ref, pairs_ref, src_ref, tgt_ref, sems):
    moves = ((count_in, count_ref), (pairs_in, pairs_ref), (src_in, src_ref), (tgt_in, tgt_ref))
    copies = [pltpu.make_async_copy(given, taken, sems.at[n]) for n, (given, taken) in enumerate(moves)]
    for copy in copies:
        copy.start()
    copies[0].wait()
    copies[1].wait()
    lists = sort_tiles(count_ref, pairs_ref)
    for n, numbers in enumerate(lists):
        for tile in range(SIDE):
            at = 2 * PART + SIDE * n + tile
            out_ref[at:at + 1, :] = numbers[:, tile * LANES:(tile + 1) * LANES]
    for n, ref in enumerate((tgt_ref, src_ref)):
        copies[3 - n].wait()
        for block in range(BLOCKS):
            for side in range(2):
                lanes = pl.ds((2 * block + side) * LANES, LANES)
                out_ref[pl.ds(n * PART + side * BLOCKS + block, 6, stride=2 * BLOCKS), :] = ref[:, lanes]


def split3(value):
    first = value.astype(jnp.bfloat16).astype(jnp.float32)
    rest = value - first
    second = rest.astype(jnp.bfloat16).astype(jnp.float32)
    return first, second, rest - second


def squares(parts):
    return parts[0] * parts[0] + parts[1] * parts[1] + parts[2] * parts[2]


def put(ref, count, first, height, row, value):
    for side in range(2):
        start = (side * count + first) * height + row
        ref[pl.ds(start, BLOCKS, stride=height), :] = value[side * BLOCKS:(side + 1) * BLOCKS]


def component(ref, base, row):
    return ref[base + row * 2 * BLOCKS:base + (row + 1) * 2 * BLOCKS, :]


def both(ref, count, block, pitch, height):
    return jnp.concatenate([ref[pl.ds((side * count + block) * pitch, height), :] for side in range(2)], axis=1)


def list_tiles(across, codes_ref):
    me = lax.axis_index("shard")
    here_x, here_y = shift(me, 2), low_bits(me, 3)
    size = SIDE * SIDE
    sub = lax.broadcasted_iota(jnp.int32, (size, size), 0)
    along = lax.broadcasted_iota(jnp.int32, (size, size), 1)
    same = (shift(sub, 2) == shift(along, 2)).astype(jnp.float32).astype(jnp.bfloat16)
    lane = lax.broadcasted_iota(jnp.int32, (size, LANES), 1)
    for p, ref in enumerate(across):
        row = ref[PART:PART + size, :].astype(jnp.int32) - 1
        col = ref[PART + size:PART + 2 * size, :].astype(jnp.int32)
        local = low_bits(col, 127)
        key = jnp.where(row < 0, 1000, taker(row, local))
        rindex = BLOCKS * low_bits(here_y - shift(row, 3), 3) + low_bits(row, 7)
        cindex = ROWS * shift(col, 7) + BLOCKS * low_bits(here_x - shift(local, 5), 3) + low_bits(local, 7)
        codes_ref[p * size:(p + 1) * size, :] = rindex * 128 + cindex
        before = jnp.sum((key < me).astype(jnp.float32), axis=1, keepdims=True)
        many = jnp.sum((key == me).astype(jnp.float32), axis=1, keepdims=True)
        both_counts = jnp.where(lane == 0, before, many).astype(jnp.bfloat16)
        both_counts = jnp.dot(same, both_counts, preferred_element_type=jnp.float32)
        codes_ref[(SIDE + p) * size:(SIDE + p + 1) * size, :] = both_counts.astype(jnp.int32)


def flatten(lists_ref, flat_ref):
    def sender(s, total):
        low = lists_ref[SIDE * (SIDE * SIDE + s), 0]
        count = lists_ref[SIDE * (SIDE * SIDE + s), 1]

        def move(step, carry):
            for u in range(8):
                k = low + step * 8 + u
                flat_ref[total + step * 8 + u] = lists_ref[SIDE * s + shift(k, 7), low_bits(k, 127)]
            return carry

        lax.fori_loop(0, shift(count + 7, 3), move, 0)
        return total + count

    total = lax.fori_loop(0, SIDE * SIDE, sender, jnp.int32(0))
    for k in range(UNROLL):
        flat_ref[total + k] = jnp.int32(-1)
    return total


def row_operand(across, rowa_ref, aexp_ref):
    nil = jnp.zeros((2 * BLOCKS, LANES), jnp.float32)
    for p, ref in enumerate(across):
        center = [component(ref, 0, a) for a in range(3)]
        parts = [split3(c * LOG2E) for c in center]
        norms = split3(squares(center) * (-0.5 * LOG2E))
        first = p * BLOCKS
        for k, level in enumerate((0, 0, 1, 1, 0, 2)):
            for a in range(3):
                put(rowa_ref, ROWS, first, KPITCH, 3 * k + a, parts[a][level])
        for k in range(3):
            put(rowa_ref, ROWS, first, KPITCH, 18 + k, norms[k])
            put(rowa_ref, ROWS, first, KPITCH, 21 + k, nil + 1.0)
        for k in range(24, KEXP):
            put(rowa_ref, ROWS, first, KPITCH, k, nil)
    for block in range(ROWS):
        aexp_ref[block] = both(rowa_ref, ROWS, block, KPITCH, KEXP).astype(jnp.bfloat16)


def column_operands(columns, weights, colb_ref, colf_ref):
    nil = jnp.zeros((2 * BLOCKS, LANES), jnp.float32)
    for array, (places, weight) in enumerate(zip(columns, weights)):
        for x, (ref, base) in enumerate(places):
            first = array * ROWS + x * BLOCKS
            center = [component(ref, base, a) for a in range(3)]
            tangent = [component(ref, base, 3 + a) for a in range(3)]
            parts = [split3(c) for c in center]
            norms = split3(squares(center) * (-0.5 * LOG2E))
            for k, level in enumerate((0, 1, 0, 1, 2, 0)):
                for a in range(3):
                    put(colb_ref, COLS + 1, first, KPITCH, 3 * k + a, parts[a][level])
            for k in range(3):
                put(colb_ref, COLS + 1, first, KPITCH, 18 + k, nil + 1.0)
                put(colb_ref, COLS + 1, first, KPITCH, 21 + k, norms[k])
            for k in range(24, KEXP):
                put(colb_ref, COLS + 1, first, KPITCH, k, nil)
            scale = weight / jnp.sqrt(squares(tangent))
            for n, (a, b) in enumerate(PAIRS):
                moment = tangent[a] * tangent[b] * scale
                put(colf_ref, COLS + 1, first, FPITCH, n, moment)
                for c in range(3):
                    put(colf_ref, COLS + 1, first, FPITCH, 6 * (c + 1) + n, moment * center[c])
    for side in range(2):
        blank = (side + 1) * (COLS + 1) - 1
        colb_ref[blank * KPITCH:blank * KPITCH + KEXP, :] = jnp.zeros((KEXP, LANES), jnp.float32)
        colf_ref[blank * FPITCH:blank * FPITCH + FEATS, :] = jnp.zeros((FEATS, LANES), jnp.float32)


def add_tiles(total, flat_ref, colb_ref, colf_ref, aexp_ref, acc_ref):
    def turn(begin, many):
        for k in range(many):
            code = flat_ref[begin + k]
            dead = code < 0
            r = jnp.where(dead, 0, lax.shift_right_logical(code, 7))
            q = jnp.where(dead, COLS, low_bits(code, 127))
            turned = both(colb_ref, COLS + 1, q, KPITCH, KEXP).T.astype(jnp.bfloat16)
            expo = jnp.dot(turned, aexp_ref[r], preferred_element_type=jnp.float32)
            value = jnp.exp2(expo)
            high = value.astype(jnp.bfloat16)
            low = (value - high.astype(jnp.float32)).astype(jnp.bfloat16)
            feats = both(colf_ref, COLS + 1, q, FPITCH, FEATS)
            upper = feats.astype(jnp.bfloat16).astype(jnp.float32)
            feats = jnp.concatenate([upper, feats - upper], axis=0).astype(jnp.bfloat16)
            got = jnp.dot(feats, high, preferred_element_type=jnp.float32)
            extra = jnp.dot(feats[0:32], low, preferred_element_type=jnp.float32)
            got = jnp.concatenate([got[0:FEATS] + extra[0:FEATS], got[FEATS:]], axis=0)
            for side in range(2):
                part = pl.ds((side * ROWS + r) * APITCH, 2 * FEATS)
                acc_ref[part, :] += got[:, side * LANES:(side + 1) * LANES]

    turns = lax.div(total + (UNROLL - sum(TAILS) - 1), UNROLL)
    rest = total - turns * UNROLL

    @pl.loop(0, turns)
    def _(step):
        turn(step * UNROLL, UNROLL)

    @pl.when(rest > TAILS[1])
    def _():
        turn(turns * UNROLL, TAILS[0])

    @pl.when((rest > 0) & (low_bits(rest - 1, TAILS[1]) == 0))
    def _():
        turn(turns * UNROLL + jnp.where(rest > TAILS[1], TAILS[0], 0), TAILS[1])


def keep_kernel(send_ref, out_ref):
    out_ref[...] = send_ref[...]


def split_kernel(along0, along1, along2, along3, shared_ref, across_ref):
    across_ref[0:PART, :] = along0[PART:2 * PART, :]
    for x, ref in enumerate((along0, along1, along2, along3)):
        shared_ref[x * PART:(x + 1) * PART, :] = ref[0:PART, :]
        for n in range(2):
            to = PART + SIDE * (SIDE * n + x)
            across_ref[to:to + SIDE, :] = ref[2 * PART + SIDE * n:2 * PART + SIDE * (n + 1), :]


def tile_kernel(
    along0, along1, along2, along3, near_ref, far_ref, across0, across1, across2, across3, out0, out1, out2, out3,
    codes_ref, colb_ref, colf_ref, rowa_ref, aexp_ref, acc_ref, lists_ref, flat_ref, sem,
):
    across = (across0, across1, across2, across3)
    list_tiles(across, codes_ref)
    copy = pltpu.make_async_copy(codes_ref, lists_ref, sem)
    copy.start()
    row_operand(across, rowa_ref, aexp_ref)
    along = (along0, along1, along2, along3)
    columns = [[(ref, base) for ref in along] for base in (PART, 0)]
    columns += [[(ref, x * PART) for x in range(SIDE)] for ref in (near_ref, far_ref)]
    column_operands(columns, (1.0, -2.0, -2.0, -2.0), colb_ref, colf_ref)
    acc_ref[...] = jnp.zeros(acc_ref.shape, jnp.float32)
    copy.wait()
    add_tiles(flatten(lists_ref, flat_ref), flat_ref, colb_ref, colf_ref, aexp_ref, acc_ref)

    for p, (ref, out_ref) in enumerate(zip(across, (out0, out1, out2, out3))):
        center = [component(ref, 0, a) for a in range(3)]
        tangent = [component(ref, 0, 3 + a) for a in range(3)]

        def moment(f):
            halves = []
            for side in range(2):
                start = (side * ROWS + p * BLOCKS) * APITCH + f
                high = acc_ref[pl.ds(start, BLOCKS, stride=APITCH), :]
                halves.append(high + acc_ref[pl.ds(start + FEATS, BLOCKS, stride=APITCH), :])
            return jnp.concatenate(halves, axis=0)

        square = squares(tangent)
        inverse = 1.0 / jnp.sqrt(square)

        def form(offset):
            m = [moment(offset + n) for n in range(6)]
            y = [sum(m[PLACE[a, b]] * tangent[b] for b in range(3)) for a in range(3)]
            return y, (y[0] * tangent[0] + y[1] * tangent[1] + y[2] * tangent[2]) * inverse

        def emit(row, value):
            out_ref[row * 2 * BLOCKS:(row + 1) * 2 * BLOCKS, :] = value * (1.0 / B)

        turned, total_k = form(0)
        ratio = total_k / square
        for a in range(3):
            _, pull = form(6 * (a + 1))
            emit(a, pull - center[a] * total_k)
            emit(3 + a, 2.0 * inverse * turned[a] - tangent[a] * ratio)


def sum_kernel(part0, part1, part2, part3, out_ref, total_ref):
    total_ref[...] = (part0[...] + part1[...]) + (part2[...] + part3[...])
    for block in range(BLOCKS):
        for side in range(2):
            lanes = pl.ds((2 * block + side) * LANES, LANES)
            out_ref[:, lanes] = total_ref[pl.ds(side * BLOCKS + block, 6, stride=2 * BLOCKS), :]


CODES = (2 * SIDE * SIDE * SIDE, LANES)
ACC = (2 * ROWS * APITCH, LANES)
COLB = (2 * (COLS + 1) * KPITCH, LANES)
COLF = (2 * (COLS + 1) * FPITCH, LANES)


def array(shape, dtype=jnp.float32):
    return jax.ShapeDtypeStruct(shape, dtype)


def call(kernel, name, out, inputs, scratch=(), flops=0, hbm=False, limit=VMEM_LIMIT):
    vmem = pl.BlockSpec(memory_space=pltpu.VMEM)
    given = pl.BlockSpec(memory_space=pl.ANY) if hbm else vmem
    return pl.pallas_call(
        kernel,
        out_shape=out,
        in_specs=[given] * len(inputs),
        out_specs=jax.tree.map(lambda _: vmem, out),
        scratch_shapes=list(scratch),
        compiler_params=pltpu.CompilerParams(vmem_limit_bytes=limit),
        cost_estimate=pl.CostEstimate(flops=flops, bytes_accessed=1 << 20, transcendentals=0) if flops else None,
        name=name,
    )(*inputs)


def tiles(along, near, far, across):
    scratch = [
        pltpu.VMEM(CODES, jnp.int32),
        pltpu.VMEM(COLB, jnp.float32),
        pltpu.VMEM(COLF, jnp.float32),
        pltpu.VMEM((2 * ROWS * KPITCH, LANES), jnp.float32),
        pltpu.VMEM((ROWS, KEXP, B), jnp.bfloat16),
        pltpu.VMEM(ACC, jnp.float32),
        pltpu.SMEM(CODES, jnp.int32),
        pltpu.SMEM((SIDE * SIDE * 512 + 128,), jnp.int32),
        pltpu.SemaphoreType.DMA,
    ]
    out = (array((PART, LANES)),) * SIDE
    return call(tile_kernel, "tile_gradients", out, (*along, near, far, *across), scratch, flops=10**10)


def per_device(source, target, tile_pairs, tile_counts):
    groups = lax.axis_size("bundle")
    chips = groups // 2
    within = [(g, g ^ 1) for g in range(groups)]
    between = [(2 * z + 1, 2 * z + 2) for z in range(chips - 1)] + [(2 * z + 2, 2 * z + 1) for z in range(chips - 1)]

    def along_x(step):
        return [(SIDE * x + y, SIDE * ((x + step) % SIDE) + y) for x in range(SIDE) for y in range(SIDE)]

    def along_y(step):
        return [(SIDE * x + y, SIDE * x + (y + step) % SIDE) for x in range(SIDE) for y in range(SIDE)]

    slots = tile_pairs.shape[0]
    scratch = [
        pltpu.SMEM(tile_counts.shape, jnp.int32),
        pltpu.VMEM((2, slots), jnp.int32),
        pltpu.VMEM(source.shape, jnp.float32),
        pltpu.VMEM(target.shape, jnp.float32),
        pltpu.SemaphoreType.DMA((4,)),
    ]
    send = call(
        pack_kernel, "sort_and_pack", array((PAYLOAD, LANES)), (tile_counts, tile_pairs.T, source, target),
        scratch, hbm=True, limit=PACK_LIMIT,
    )
    passed = [lax.ppermute(send, "shard", along_x(step)) for step in range(1, SIDE)]
    along = (call(keep_kernel, "keep", array((PAYLOAD, LANES)), (send,), flops=10**9), *passed)
    shared, across = call(split_kernel, "split", (array((SIDE * PART, LANES)), array((ACROSS, LANES))), along)
    near = lax.ppermute(shared, "bundle", within)
    far = lax.ppermute(shared, "bundle", between)
    passed = [lax.ppermute(across, "shard", along_y(step)) for step in range(1, SIDE)]
    parts = tiles(along, near, far, (across, *passed))
    back = [lax.ppermute(parts[step], "shard", along_y(-step)) for step in range(1, SIDE)]
    return call(
        sum_kernel, "add_parts", array((6, 8 * B)), (parts[0], *back), [pltpu.VMEM((PART, LANES), jnp.float32)]
    )


def solution(mesh):
    in_specs = (
        P(None, ("bundle", "shard")),
        P(None, ("bundle", "shard")),
        P(("bundle", "shard"), None),
        P(("bundle", "shard")),
    )
    out_specs = P(None, ("bundle", "shard"))
    return jax.shard_map(
        per_device, mesh=mesh, in_specs=in_specs, out_specs=out_specs, check_vma=False
    )
```

```python
import jax
import jax.numpy as jnp
from jax import lax
from jax.experimental import pallas as pl
from jax.experimental.pallas import tpu as pltpu
from jax.sharding import PartitionSpec as P

B = 256
LANES = 128
LOG2E = 1.4426950408889634
SIDE = 4
BLOCKS = 8
PART = 6 * 2 * BLOCKS
LISTS = 8
AT_ONCE = 12
FARTHEST_FIRST = (2, 1, 3)
PAYLOAD = 2 * PART + LISTS
ACROSS = PART + SIDE * LISTS
KEXP = 32
KPITCH = 33
FEATS = 24
FPITCH = 25
APITCH = 49
ROWS = SIDE * BLOCKS
COLS = 4 * ROWS
UNROLL = 32
TAILS = (16, 8)
VMEM_LIMIT = 40 * 1024 * 1024
PACK_LIMIT = 60 * 1024 * 1024

NT = (((1,), (1,)), ((), ()))
PAIRS = ((0, 0), (0, 1), (0, 2), (1, 1), (1, 2), (2, 2))
PLACE = {(a, b): n for n, pair in enumerate(PAIRS) for a, b in (pair, pair[::-1])}


def shift(value, bits):
    return lax.shift_right_arithmetic(value, bits)


def low_bits(value, mask):
    return lax.bitwise_and(value, mask)


def taker(row, col):
    return SIDE * shift(row, 5) + low_bits(shift(col, 3), 3)


def sort_tiles(count_ref, pairs_ref):
    slots = pairs_ref.shape[1]
    group = lax.axis_index("bundle")
    row = pairs_ref[0:1, :] - group * 128
    col = pairs_ref[1:2, :]
    total_blocks = 8 * 128
    is_source = col < total_blocks
    local = col - jnp.where(is_source, group * 128, total_blocks + (group - 1) * 128)
    step = shift(local, 7)
    step = jnp.where(low_bits(group, 1) == 1, step, 2 - step)
    array = jnp.where(is_source, 0, jnp.where(step == 1, 1, jnp.where(step == 0, 2, 3)))
    local = low_bits(local, 127)
    live = lax.broadcasted_iota(jnp.int32, (1, slots), 1) < count_ref[0]
    key = jnp.where(live, taker(row, local), 1000)

    lane = lax.broadcasted_iota(jnp.int32, (slots, slots), 1)
    sub = lax.broadcasted_iota(jnp.int32, (slots, slots), 0)
    earlier = (sub < lane).astype(jnp.float32).astype(jnp.bfloat16)
    owner = lax.broadcasted_iota(jnp.int32, (SIDE * SIDE, slots), 0)
    mine = (owner == key).astype(jnp.float32)
    rank = jnp.dot(mine.astype(jnp.bfloat16), earlier, preferred_element_type=jnp.float32)
    start = jnp.sum((owner > key).astype(jnp.float32), axis=1, keepdims=True)
    place = jnp.sum(mine * (rank + start), axis=0, keepdims=True).astype(jnp.int32)
    place = jnp.where(live, place, -1)
    onehot = (sub == place).astype(jnp.float32).astype(jnp.bfloat16)
    parts = [part.astype(jnp.float32) for part in (row + 1, array, local)]
    parts = jnp.concatenate(parts + [jnp.zeros((5, slots), jnp.float32)], axis=0)
    moved = lax.dot_general(parts.astype(jnp.bfloat16), onehot, NT, preferred_element_type=jnp.float32)
    return moved[0:1], moved[1:2] * 128.0 + moved[2:3]


def pack_kernel(count_in, pairs_in, src_in, tgt_in, out_ref, count_ref, pairs_ref, src_ref, tgt_ref, sems):
    moves = ((count_in, count_ref), (pairs_in, pairs_ref), (src_in, src_ref), (tgt_in, tgt_ref))
    copies = [pltpu.make_async_copy(given, taken, sems.at[n]) for n, (given, taken) in enumerate(moves)]
    for copy in copies:
        copy.start()
    copies[0].wait()
    copies[1].wait()
    lists = sort_tiles(count_ref, pairs_ref)
    for n, numbers in enumerate(lists):
        for tile in range(SIDE):
            at = 2 * PART + SIDE * n + tile
            out_ref[at:at + 1, :] = numbers[:, tile * LANES:(tile + 1) * LANES]
    for n, ref in enumerate((tgt_ref, src_ref)):
        copies[3 - n].wait()
        for block in range(BLOCKS):
            for side in range(2):
                lanes = pl.ds((2 * block + side) * LANES, LANES)
                out_ref[pl.ds(n * PART + side * BLOCKS + block, 6, stride=2 * BLOCKS), :] = ref[:, lanes]


def split3(value):
    first = value.astype(jnp.bfloat16).astype(jnp.float32)
    rest = value - first
    second = rest.astype(jnp.bfloat16).astype(jnp.float32)
    return first, second, rest - second


def squares(parts):
    return parts[0] * parts[0] + parts[1] * parts[1] + parts[2] * parts[2]


def put(ref, count, first, height, row, value):
    for side in range(2):
        start = (side * count + first) * height + row
        ref[pl.ds(start, BLOCKS, stride=height), :] = value[side * BLOCKS:(side + 1) * BLOCKS]


def component(ref, base, row):
    return ref[base + row * 2 * BLOCKS:base + (row + 1) * 2 * BLOCKS, :]


def both(ref, count, block, pitch, height):
    return jnp.concatenate([ref[pl.ds((side * count + block) * pitch, height), :] for side in range(2)], axis=1)


def list_tiles(across, codes_ref):
    me = lax.axis_index("shard")
    here_x, here_y = shift(me, 2), low_bits(me, 3)
    size = SIDE * SIDE
    sub = lax.broadcasted_iota(jnp.int32, (size, size), 0)
    along = lax.broadcasted_iota(jnp.int32, (size, size), 1)
    same = (shift(sub, 2) == shift(along, 2)).astype(jnp.float32).astype(jnp.bfloat16)
    lane = lax.broadcasted_iota(jnp.int32, (size, LANES), 1)
    counts = jnp.zeros((size, LANES), jnp.float32)
    for p, ref in enumerate(across):
        row = ref[PART:PART + size, :].astype(jnp.int32) - 1
        col = ref[PART + size:PART + 2 * size, :].astype(jnp.int32)
        local = low_bits(col, 127)
        key = jnp.where(row < 0, 1000, taker(row, local))
        rindex = BLOCKS * low_bits(here_y - shift(row, 3), 3) + low_bits(row, 7)
        cindex = ROWS * shift(col, 7) + BLOCKS * low_bits(here_x - shift(local, 5), 3) + low_bits(local, 7)
        codes_ref[p * size:(p + 1) * size, :] = rindex * 128 + cindex
        before = jnp.sum((key < me).astype(jnp.float32), axis=1, keepdims=True)
        many = jnp.sum((key == me).astype(jnp.float32), axis=1, keepdims=True)
        counts = jnp.where(lane == 2 * p, before, jnp.where(lane == 2 * p + 1, many, counts))
    counts = jnp.dot(same, counts.astype(jnp.bfloat16), preferred_element_type=jnp.float32)
    codes_ref[SIDE * size:(SIDE + 1) * size, :] = counts.astype(jnp.int32)


def flatten(lists_ref, flat_ref):
    total = jnp.int32(0)
    for s in range(SIDE * SIDE):
        p, x = divmod(s, SIDE)
        low = lists_ref[SIDE * SIDE * SIDE + SIDE * x, 2 * p]
        count = lists_ref[SIDE * SIDE * SIDE + SIDE * x, 2 * p + 1]

        def move(first, many, low=low, total=total, s=s):
            for u in range(many):
                k = low + first + u
                flat_ref[total + first + u] = lists_ref[SIDE * s + shift(k, 7), low_bits(k, 127)]

        move(0, AT_ONCE)

        @pl.loop(0, shift(jnp.maximum(count - AT_ONCE, 0) + 7, 3))
        def _(step, move=move):
            move(AT_ONCE + step * 8, 8)

        total = total + count
    for k in range(UNROLL):
        flat_ref[total + k] = jnp.int32(-1)
    return total


def row_operand(across, rowa_ref, aexp_ref):
    nil = jnp.zeros((2 * BLOCKS, LANES), jnp.float32)
    for p, ref in enumerate(across):
        center = [component(ref, 0, a) for a in range(3)]
        parts = [split3(c * LOG2E) for c in center]
        norms = split3(squares(center) * (-0.5 * LOG2E))
        first = p * BLOCKS
        for k, level in enumerate((0, 0, 1, 1, 0, 2)):
            for a in range(3):
                put(rowa_ref, ROWS, first, KPITCH, 3 * k + a, parts[a][level])
        for k in range(3):
            put(rowa_ref, ROWS, first, KPITCH, 18 + k, norms[k])
            put(rowa_ref, ROWS, first, KPITCH, 21 + k, nil + 1.0)
        for k in range(24, KEXP):
            put(rowa_ref, ROWS, first, KPITCH, k, nil)
    for block in range(ROWS):
        aexp_ref[block] = both(rowa_ref, ROWS, block, KPITCH, KEXP).astype(jnp.bfloat16)


def column_operands(columns, weights, colb_ref, colf_ref):
    nil = jnp.zeros((2 * BLOCKS, LANES), jnp.float32)
    for array, (places, weight) in enumerate(zip(columns, weights)):
        for x, (ref, base) in enumerate(places):
            first = array * ROWS + x * BLOCKS
            center = [component(ref, base, a) for a in range(3)]
            tangent = [component(ref, base, 3 + a) for a in range(3)]
            parts = [split3(c) for c in center]
            norms = split3(squares(center) * (-0.5 * LOG2E))
            for k, level in enumerate((0, 1, 0, 1, 2, 0)):
                for a in range(3):
                    put(colb_ref, COLS + 1, first, KPITCH, 3 * k + a, parts[a][level])
            for k in range(3):
                put(colb_ref, COLS + 1, first, KPITCH, 18 + k, nil + 1.0)
                put(colb_ref, COLS + 1, first, KPITCH, 21 + k, norms[k])
            for k in range(24, KEXP):
                put(colb_ref, COLS + 1, first, KPITCH, k, nil)
            scale = weight / jnp.sqrt(squares(tangent))
            for n, (a, b) in enumerate(PAIRS):
                moment = tangent[a] * tangent[b] * scale
                put(colf_ref, COLS + 1, first, FPITCH, n, moment)
                for c in range(3):
                    put(colf_ref, COLS + 1, first, FPITCH, 6 * (c + 1) + n, moment * center[c])
    for side in range(2):
        blank = (side + 1) * (COLS + 1) - 1
        colb_ref[blank * KPITCH:blank * KPITCH + KEXP, :] = jnp.zeros((KEXP, LANES), jnp.float32)
        colf_ref[blank * FPITCH:blank * FPITCH + FEATS, :] = jnp.zeros((FEATS, LANES), jnp.float32)


def add_tiles(total, flat_ref, colb_ref, colf_ref, aexp_ref, acc_ref):
    def turn(begin, many):
        for k in range(many):
            code = flat_ref[begin + k]
            dead = code < 0
            r = jnp.where(dead, 0, lax.shift_right_logical(code, 7))
            q = jnp.where(dead, COLS, low_bits(code, 127))
            turned = both(colb_ref, COLS + 1, q, KPITCH, KEXP).T.astype(jnp.bfloat16)
            expo = jnp.dot(turned, aexp_ref[r], preferred_element_type=jnp.float32)
            value = jnp.exp2(expo)
            high = value.astype(jnp.bfloat16)
            low = (value - high.astype(jnp.float32)).astype(jnp.bfloat16)
            feats = both(colf_ref, COLS + 1, q, FPITCH, FEATS)
            main = feats.astype(jnp.bfloat16)
            upper = main.astype(jnp.float32)
            feats = jnp.concatenate([upper, feats - upper], axis=0).astype(jnp.bfloat16)
            got = jnp.dot(feats, high, preferred_element_type=jnp.float32)
            extra = jnp.dot(main, low, preferred_element_type=jnp.float32)
            got = jnp.concatenate([got[0:FEATS] + extra, got[FEATS:]], axis=0)
            for side in range(2):
                part = pl.ds((side * ROWS + r) * APITCH, 2 * FEATS)
                acc_ref[part, :] += got[:, side * LANES:(side + 1) * LANES]

    turns = lax.div(total + (UNROLL - sum(TAILS) - 1), UNROLL)
    rest = total - turns * UNROLL

    @pl.loop(0, turns)
    def _(step):
        turn(step * UNROLL, UNROLL)

    @pl.when(rest > TAILS[1])
    def _():
        turn(turns * UNROLL, TAILS[0])

    @pl.when((rest > 0) & (low_bits(rest - 1, TAILS[1]) == 0))
    def _():
        turn(turns * UNROLL + jnp.where(rest > TAILS[1], TAILS[0], 0), TAILS[1])


def keep_kernel(send_ref, out_ref):
    out_ref[...] = send_ref[...]


def split_kernel(along0, along1, along2, along3, shared_ref, across_ref):
    across_ref[0:PART, :] = along0[PART:2 * PART, :]
    for x, ref in enumerate((along0, along1, along2, along3)):
        shared_ref[x * PART:(x + 1) * PART, :] = ref[0:PART, :]
        for n in range(2):
            to = PART + SIDE * (SIDE * n + x)
            across_ref[to:to + SIDE, :] = ref[2 * PART + SIDE * n:2 * PART + SIDE * (n + 1), :]


def tile_kernel(
    along0, along1, along2, along3, near_ref, far_ref, across0, across1, across2, across3, out0, out1, out2, out3,
    codes_ref, colb_ref, colf_ref, rowa_ref, aexp_ref, acc_ref, lists_ref, flat_ref, sem,
):
    across = (across0, across1, across2, across3)
    list_tiles(across, codes_ref)
    copy = pltpu.make_async_copy(codes_ref, lists_ref, sem)
    copy.start()
    row_operand(across, rowa_ref, aexp_ref)
    along = (along0, along1, along2, along3)
    columns = [[(ref, base) for ref in along] for base in (PART, 0)]
    columns += [[(ref, x * PART) for x in range(SIDE)] for ref in (near_ref, far_ref)]
    column_operands(columns, (1.0, -2.0, -2.0, -2.0), colb_ref, colf_ref)
    acc_ref[...] = jnp.zeros(acc_ref.shape, jnp.float32)
    copy.wait()
    add_tiles(flatten(lists_ref, flat_ref), flat_ref, colb_ref, colf_ref, aexp_ref, acc_ref)

    for p, (ref, out_ref) in enumerate(zip(across, (out0, out1, out2, out3))):
        center = [component(ref, 0, a) for a in range(3)]
        tangent = [component(ref, 0, 3 + a) for a in range(3)]

        def moment(f):
            halves = []
            for side in range(2):
                start = (side * ROWS + p * BLOCKS) * APITCH + f
                high = acc_ref[pl.ds(start, BLOCKS, stride=APITCH), :]
                halves.append(high + acc_ref[pl.ds(start + FEATS, BLOCKS, stride=APITCH), :])
            return jnp.concatenate(halves, axis=0)

        square = squares(tangent)
        inverse = 1.0 / jnp.sqrt(square)

        def form(offset):
            m = [moment(offset + n) for n in range(6)]
            y = [sum(m[PLACE[a, b]] * tangent[b] for b in range(3)) for a in range(3)]
            return y, (y[0] * tangent[0] + y[1] * tangent[1] + y[2] * tangent[2]) * inverse

        def emit(row, value):
            out_ref[row * 2 * BLOCKS:(row + 1) * 2 * BLOCKS, :] = value * (1.0 / B)

        turned, total_k = form(0)
        ratio = total_k / square
        for a in range(3):
            _, pull = form(6 * (a + 1))
            emit(a, pull - center[a] * total_k)
            emit(3 + a, 2.0 * inverse * turned[a] - tangent[a] * ratio)


def sum_kernel(part0, part1, part2, part3, out_ref, total_ref):
    total_ref[...] = (part0[...] + part1[...]) + (part2[...] + part3[...])
    for block in range(BLOCKS):
        for side in range(2):
            lanes = pl.ds((2 * block + side) * LANES, LANES)
            out_ref[:, lanes] = total_ref[pl.ds(side * BLOCKS + block, 6, stride=2 * BLOCKS), :]


CODES = ((SIDE + 1) * SIDE * SIDE, LANES)
ACC = (2 * ROWS * APITCH, LANES)
COLB = (2 * (COLS + 1) * KPITCH, LANES)
COLF = (2 * (COLS + 1) * FPITCH, LANES)


def array(shape, dtype=jnp.float32):
    return jax.ShapeDtypeStruct(shape, dtype)


def call(kernel, name, out, inputs, scratch=(), flops=0, hbm=False, limit=VMEM_LIMIT):
    vmem = pl.BlockSpec(memory_space=pltpu.VMEM)
    given = pl.BlockSpec(memory_space=pl.ANY) if hbm else vmem
    return pl.pallas_call(
        kernel,
        out_shape=out,
        in_specs=[given] * len(inputs),
        out_specs=jax.tree.map(lambda _: vmem, out),
        scratch_shapes=list(scratch),
        compiler_params=pltpu.CompilerParams(vmem_limit_bytes=limit),
        cost_estimate=pl.CostEstimate(flops=flops, bytes_accessed=1 << 20, transcendentals=0) if flops else None,
        name=name,
    )(*inputs)


def tiles(along, near, far, across):
    scratch = [
        pltpu.VMEM(CODES, jnp.int32),
        pltpu.VMEM(COLB, jnp.float32),
        pltpu.VMEM(COLF, jnp.float32),
        pltpu.VMEM((2 * ROWS * KPITCH, LANES), jnp.float32),
        pltpu.VMEM((ROWS, KEXP, B), jnp.bfloat16),
        pltpu.VMEM(ACC, jnp.float32),
        pltpu.SMEM(CODES, jnp.int32),
        pltpu.SMEM((SIDE * SIDE * 512 + 128,), jnp.int32),
        pltpu.SemaphoreType.DMA,
    ]
    out = (array((PART, LANES)),) * SIDE
    return call(tile_kernel, "tile_gradients", out, (*along, near, far, *across), scratch, flops=10**10)


def per_device(source, target, tile_pairs, tile_counts):
    groups = lax.axis_size("bundle")
    chips = groups // 2
    within = [(g, g ^ 1) for g in range(groups)]
    between = [(2 * z + 1, 2 * z + 2) for z in range(chips - 1)] + [(2 * z + 2, 2 * z + 1) for z in range(chips - 1)]

    def along_x(step):
        return [(SIDE * x + y, SIDE * ((x + step) % SIDE) + y) for x in range(SIDE) for y in range(SIDE)]

    def along_y(step):
        return [(SIDE * x + y, SIDE * x + (y + step) % SIDE) for x in range(SIDE) for y in range(SIDE)]

    slots = tile_pairs.shape[0]
    scratch = [
        pltpu.SMEM(tile_counts.shape, jnp.int32),
        pltpu.VMEM((2, slots), jnp.int32),
        pltpu.VMEM(source.shape, jnp.float32),
        pltpu.VMEM(target.shape, jnp.float32),
        pltpu.SemaphoreType.DMA((4,)),
    ]
    send = call(
        pack_kernel, "sort_and_pack", array((PAYLOAD, LANES)), (tile_counts, tile_pairs.T, source, target),
        scratch, hbm=True, limit=PACK_LIMIT,
    )
    passed = {step: lax.ppermute(send, "shard", along_x(step)) for step in FARTHEST_FIRST}
    along = (call(keep_kernel, "keep", array((PAYLOAD, LANES)), (send,), flops=10**9), passed[1], passed[2], passed[3])
    shared, across = call(split_kernel, "split", (array((SIDE * PART, LANES)), array((ACROSS, LANES))), along)
    near = lax.ppermute(shared, "bundle", within)
    far = lax.ppermute(shared, "bundle", between)
    passed = {step: lax.ppermute(across, "shard", along_y(step)) for step in FARTHEST_FIRST}
    parts = tiles(along, near, far, (across, passed[1], passed[2], passed[3]))
    back = [lax.ppermute(parts[step], "shard", along_y(-step)) for step in FARTHEST_FIRST]
    return call(
        sum_kernel, "add_parts", array((6, 8 * B)), (parts[0], *back), [pltpu.VMEM((PART, LANES), jnp.float32)]
    )


def solution(mesh):
    in_specs = (
        P(None, ("bundle", "shard")),
        P(None, ("bundle", "shard")),
        P(("bundle", "shard"), None),
        P(("bundle", "shard")),
    )
    out_specs = P(None, ("bundle", "shard"))
    return jax.shard_map(
        per_device, mesh=mesh, in_specs=in_specs, out_specs=out_specs, check_vma=False
    )
```

```python
import jax
import jax.numpy as jnp
from jax import lax
from jax.experimental import pallas as pl
from jax.experimental.pallas import tpu as pltpu
from jax.sharding import PartitionSpec as P

B = 256
LANES = 128
LOG2E = 1.4426950408889634
SIDE = 4
BLOCKS = 8
PART = 6 * 2 * BLOCKS
LISTS = 8
AT_ONCE = 12
FARTHEST_FIRST = (2, 1, 3)
PAYLOAD = 2 * PART + LISTS
ACROSS = PART + SIDE * LISTS
KEXP = 32
KPITCH = 33
FEATS = 24
FPITCH = 25
APITCH = 49
ROWS = SIDE * BLOCKS
COLS = 4 * ROWS
UNROLL = 64
TAILS = (32, 16, 8)
VMEM_LIMIT = 40 * 1024 * 1024
PACK_LIMIT = 60 * 1024 * 1024

NT = (((1,), (1,)), ((), ()))
PAIRS = ((0, 0), (0, 1), (0, 2), (1, 1), (1, 2), (2, 2))
PLACE = {(a, b): n for n, pair in enumerate(PAIRS) for a, b in (pair, pair[::-1])}


def shift(value, bits):
    return lax.shift_right_arithmetic(value, bits)


def low_bits(value, mask):
    return lax.bitwise_and(value, mask)


def taker(row, col):
    return SIDE * shift(row, 5) + low_bits(shift(col, 3), 3)


def sort_tiles(count_ref, pairs_ref):
    slots = pairs_ref.shape[1]
    group = lax.axis_index("bundle")
    row = pairs_ref[0:1, :] - group * 128
    col = pairs_ref[1:2, :]
    total_blocks = 8 * 128
    is_source = col < total_blocks
    local = col - jnp.where(is_source, group * 128, total_blocks + (group - 1) * 128)
    step = shift(local, 7)
    step = jnp.where(low_bits(group, 1) == 1, step, 2 - step)
    array = jnp.where(is_source, 0, jnp.where(step == 1, 1, jnp.where(step == 0, 2, 3)))
    local = low_bits(local, 127)
    live = lax.broadcasted_iota(jnp.int32, (1, slots), 1) < count_ref[0]
    key = jnp.where(live, taker(row, local), 1000)

    lane = lax.broadcasted_iota(jnp.int32, (slots, slots), 1)
    sub = lax.broadcasted_iota(jnp.int32, (slots, slots), 0)
    earlier = (sub < lane).astype(jnp.float32).astype(jnp.bfloat16)
    owner = lax.broadcasted_iota(jnp.int32, (SIDE * SIDE, slots), 0)
    mine = (owner == key).astype(jnp.float32)
    rank = jnp.dot(mine.astype(jnp.bfloat16), earlier, preferred_element_type=jnp.float32)
    start = jnp.sum((owner > key).astype(jnp.float32), axis=1, keepdims=True)
    place = jnp.sum(mine * (rank + start), axis=0, keepdims=True).astype(jnp.int32)
    place = jnp.where(live, place, -1)
    onehot = (sub == place).astype(jnp.float32).astype(jnp.bfloat16)
    parts = [part.astype(jnp.float32) for part in (row + 1, array, local)]
    parts = jnp.concatenate(parts + [jnp.zeros((5, slots), jnp.float32)], axis=0)
    moved = lax.dot_general(parts.astype(jnp.bfloat16), onehot, NT, preferred_element_type=jnp.float32)
    return moved[0:1], moved[1:2] * 128.0 + moved[2:3]


def pack_kernel(count_in, pairs_in, src_in, tgt_in, out_ref, count_ref, pairs_ref, src_ref, tgt_ref, sems):
    moves = ((count_in, count_ref), (pairs_in, pairs_ref), (src_in, src_ref), (tgt_in, tgt_ref))
    copies = [pltpu.make_async_copy(given, taken, sems.at[n]) for n, (given, taken) in enumerate(moves)]
    for copy in copies:
        copy.start()
    copies[0].wait()
    copies[1].wait()
    lists = sort_tiles(count_ref, pairs_ref)
    for n, numbers in enumerate(lists):
        for tile in range(SIDE):
            at = 2 * PART + SIDE * n + tile
            out_ref[at:at + 1, :] = numbers[:, tile * LANES:(tile + 1) * LANES]
    for n, ref in enumerate((tgt_ref, src_ref)):
        copies[3 - n].wait()
        for block in range(BLOCKS):
            for side in range(2):
                lanes = pl.ds((2 * block + side) * LANES, LANES)
                out_ref[pl.ds(n * PART + side * BLOCKS + block, 6, stride=2 * BLOCKS), :] = ref[:, lanes]


def split3(value):
    first = value.astype(jnp.bfloat16).astype(jnp.float32)
    rest = value - first
    second = rest.astype(jnp.bfloat16).astype(jnp.float32)
    return first, second, rest - second


def squares(parts):
    return parts[0] * parts[0] + parts[1] * parts[1] + parts[2] * parts[2]


def put(ref, count, first, height, row, value):
    for side in range(2):
        start = (side * count + first) * height + row
        ref[pl.ds(start, BLOCKS, stride=height), :] = value[side * BLOCKS:(side + 1) * BLOCKS]


def component(ref, base, row):
    return ref[base + row * 2 * BLOCKS:base + (row + 1) * 2 * BLOCKS, :]


def both(ref, count, block, pitch, height):
    return jnp.concatenate([ref[pl.ds((side * count + block) * pitch, height), :] for side in range(2)], axis=1)


def list_tiles(across, codes_ref):
    me = lax.axis_index("shard")
    here_x, here_y = shift(me, 2), low_bits(me, 3)
    size = SIDE * SIDE
    sub = lax.broadcasted_iota(jnp.int32, (size, size), 0)
    along = lax.broadcasted_iota(jnp.int32, (size, size), 1)
    same = (shift(sub, 2) == shift(along, 2)).astype(jnp.float32).astype(jnp.bfloat16)
    lane = lax.broadcasted_iota(jnp.int32, (size, LANES), 1)
    counts = jnp.zeros((size, LANES), jnp.float32)
    for p, ref in enumerate(across):
        row = ref[PART:PART + size, :].astype(jnp.int32) - 1
        col = ref[PART + size:PART + 2 * size, :].astype(jnp.int32)
        local = low_bits(col, 127)
        key = jnp.where(row < 0, 1000, taker(row, local))
        rindex = BLOCKS * low_bits(here_y - shift(row, 3), 3) + low_bits(row, 7)
        cindex = ROWS * shift(col, 7) + BLOCKS * low_bits(here_x - shift(local, 5), 3) + low_bits(local, 7)
        codes_ref[p * size:(p + 1) * size, :] = rindex * 128 + cindex
        before = jnp.sum((key < me).astype(jnp.float32), axis=1, keepdims=True)
        many = jnp.sum((key == me).astype(jnp.float32), axis=1, keepdims=True)
        counts = jnp.where(lane == 2 * p, before, jnp.where(lane == 2 * p + 1, many, counts))
    counts = jnp.dot(same, counts.astype(jnp.bfloat16), preferred_element_type=jnp.float32)
    codes_ref[SIDE * size:(SIDE + 1) * size, :] = counts.astype(jnp.int32)


def flatten(lists_ref, flat_ref):
    total = jnp.int32(0)
    for s in range(SIDE * SIDE):
        p, x = divmod(s, SIDE)
        low = lists_ref[SIDE * SIDE * SIDE + SIDE * x, 2 * p]
        count = lists_ref[SIDE * SIDE * SIDE + SIDE * x, 2 * p + 1]

        def move(first, many, low=low, total=total, s=s):
            for u in range(many):
                k = low + first + u
                flat_ref[total + first + u] = lists_ref[SIDE * s + shift(k, 7), low_bits(k, 127)]

        move(0, AT_ONCE)

        @pl.loop(0, shift(jnp.maximum(count - AT_ONCE, 0) + 7, 3))
        def _(step, move=move):
            move(AT_ONCE + step * 8, 8)

        total = total + count
    for k in range(UNROLL):
        flat_ref[total + k] = jnp.int32(-1)
    return total


def row_operand(across, rowa_ref, aexp_ref):
    nil = jnp.zeros((2 * BLOCKS, LANES), jnp.float32)
    for p, ref in enumerate(across):
        center = [component(ref, 0, a) for a in range(3)]
        parts = [split3(c * LOG2E) for c in center]
        norms = split3(squares(center) * (-0.5 * LOG2E))
        first = p * BLOCKS
        for k, level in enumerate((0, 0, 1, 1, 0, 2)):
            for a in range(3):
                put(rowa_ref, ROWS, first, KPITCH, 3 * k + a, parts[a][level])
        for k in range(3):
            put(rowa_ref, ROWS, first, KPITCH, 18 + k, norms[k])
            put(rowa_ref, ROWS, first, KPITCH, 21 + k, nil + 1.0)
        for k in range(24, KEXP):
            put(rowa_ref, ROWS, first, KPITCH, k, nil)
    for block in range(ROWS):
        aexp_ref[block] = both(rowa_ref, ROWS, block, KPITCH, KEXP).astype(jnp.bfloat16)


def column_operands(columns, weights, colb_ref, colf_ref):
    nil = jnp.zeros((2 * BLOCKS, LANES), jnp.float32)
    for array, (places, weight) in enumerate(zip(columns, weights)):
        for x, (ref, base) in enumerate(places):
            first = array * ROWS + x * BLOCKS
            center = [component(ref, base, a) for a in range(3)]
            tangent = [component(ref, base, 3 + a) for a in range(3)]
            parts = [split3(c) for c in center]
            norms = split3(squares(center) * (-0.5 * LOG2E))
            for k, level in enumerate((0, 1, 0, 1, 2, 0)):
                for a in range(3):
                    put(colb_ref, COLS + 1, first, KPITCH, 3 * k + a, parts[a][level])
            for k in range(3):
                put(colb_ref, COLS + 1, first, KPITCH, 18 + k, nil + 1.0)
                put(colb_ref, COLS + 1, first, KPITCH, 21 + k, norms[k])
            for k in range(24, KEXP):
                put(colb_ref, COLS + 1, first, KPITCH, k, nil)
            scale = weight / jnp.sqrt(squares(tangent))
            for n, (a, b) in enumerate(PAIRS):
                moment = tangent[a] * tangent[b] * scale
                put(colf_ref, COLS + 1, first, FPITCH, n, moment)
                for c in range(3):
                    put(colf_ref, COLS + 1, first, FPITCH, 6 * (c + 1) + n, moment * center[c])
    for side in range(2):
        blank = (side + 1) * (COLS + 1) - 1
        colb_ref[blank * KPITCH:blank * KPITCH + KEXP, :] = jnp.zeros((KEXP, LANES), jnp.float32)
        colf_ref[blank * FPITCH:blank * FPITCH + FEATS, :] = jnp.zeros((FEATS, LANES), jnp.float32)


def add_tiles(total, flat_ref, colb_ref, colf_ref, aexp_ref, acc_ref):
    def turn(begin, many):
        for k in range(many):
            code = flat_ref[begin + k]
            dead = code < 0
            r = jnp.where(dead, 0, lax.shift_right_logical(code, 7))
            q = jnp.where(dead, COLS, low_bits(code, 127))
            turned = both(colb_ref, COLS + 1, q, KPITCH, KEXP).T.astype(jnp.bfloat16)
            expo = jnp.dot(turned, aexp_ref[r], preferred_element_type=jnp.float32)
            value = jnp.exp2(expo)
            high = value.astype(jnp.bfloat16)
            low = (value - high.astype(jnp.float32)).astype(jnp.bfloat16)
            feats = both(colf_ref, COLS + 1, q, FPITCH, FEATS)
            main = feats.astype(jnp.bfloat16)
            upper = main.astype(jnp.float32)
            feats = jnp.concatenate([upper, feats - upper], axis=0).astype(jnp.bfloat16)
            got = jnp.dot(feats, high, preferred_element_type=jnp.float32)
            extra = jnp.dot(main, low, preferred_element_type=jnp.float32)
            got = jnp.concatenate([got[0:FEATS] + extra, got[FEATS:]], axis=0)
            for side in range(2):
                part = pl.ds((side * ROWS + r) * APITCH, 2 * FEATS)
                acc_ref[part, :] += got[:, side * LANES:(side + 1) * LANES]

    turns = lax.div(total + 7, UNROLL)
    eighths = shift(jnp.maximum(total - turns * UNROLL, 0) + 7, 3)

    @pl.loop(0, turns)
    def _(step):
        turn(step * UNROLL, UNROLL)

    for many in TAILS:
        done = eighths - low_bits(eighths, many // 4 - 1)

        @pl.when(low_bits(eighths, many // 8) > 0)
        def _(many=many, done=done):
            turn(turns * UNROLL + 8 * done, many)


def keep_kernel(send_ref, out_ref):
    out_ref[...] = send_ref[...]


def split_kernel(along0, along1, along2, along3, shared_ref, across_ref):
    across_ref[0:PART, :] = along0[PART:2 * PART, :]
    for x, ref in enumerate((along0, along1, along2, along3)):
        shared_ref[x * PART:(x + 1) * PART, :] = ref[0:PART, :]
        for n in range(2):
            to = PART + SIDE * (SIDE * n + x)
            across_ref[to:to + SIDE, :] = ref[2 * PART + SIDE * n:2 * PART + SIDE * (n + 1), :]


def tile_kernel(
    along0, along1, along2, along3, near_ref, far_ref, across0, across1, across2, across3, out0, out1, out2, out3,
    codes_ref, colb_ref, colf_ref, rowa_ref, aexp_ref, acc_ref, lists_ref, flat_ref, sem,
):
    across = (across0, across1, across2, across3)
    list_tiles(across, codes_ref)
    copy = pltpu.make_async_copy(codes_ref, lists_ref, sem)
    copy.start()
    row_operand(across, rowa_ref, aexp_ref)
    along = (along0, along1, along2, along3)
    columns = [[(ref, base) for ref in along] for base in (PART, 0)]
    columns += [[(ref, x * PART) for x in range(SIDE)] for ref in (near_ref, far_ref)]
    column_operands(columns, (1.0, -2.0, -2.0, -2.0), colb_ref, colf_ref)
    acc_ref[...] = jnp.zeros(acc_ref.shape, jnp.float32)
    copy.wait()
    add_tiles(flatten(lists_ref, flat_ref), flat_ref, colb_ref, colf_ref, aexp_ref, acc_ref)

    for p, (ref, out_ref) in enumerate(zip(across, (out0, out1, out2, out3))):
        center = [component(ref, 0, a) for a in range(3)]
        tangent = [component(ref, 0, 3 + a) for a in range(3)]

        def moment(f):
            halves = []
            for side in range(2):
                start = (side * ROWS + p * BLOCKS) * APITCH + f
                high = acc_ref[pl.ds(start, BLOCKS, stride=APITCH), :]
                halves.append(high + acc_ref[pl.ds(start + FEATS, BLOCKS, stride=APITCH), :])
            return jnp.concatenate(halves, axis=0)

        square = squares(tangent)
        inverse = 1.0 / jnp.sqrt(square)

        def form(offset):
            m = [moment(offset + n) for n in range(6)]
            y = [sum(m[PLACE[a, b]] * tangent[b] for b in range(3)) for a in range(3)]
            return y, (y[0] * tangent[0] + y[1] * tangent[1] + y[2] * tangent[2]) * inverse

        def emit(row, value):
            out_ref[row * 2 * BLOCKS:(row + 1) * 2 * BLOCKS, :] = value * (1.0 / B)

        turned, total_k = form(0)
        ratio = total_k / square
        for a in range(3):
            _, pull = form(6 * (a + 1))
            emit(a, pull - center[a] * total_k)
            emit(3 + a, 2.0 * inverse * turned[a] - tangent[a] * ratio)


def sum_kernel(part0, part1, part2, part3, out_ref, total_ref):
    total_ref[...] = (part0[...] + part1[...]) + (part2[...] + part3[...])
    for block in range(BLOCKS):
        for side in range(2):
            lanes = pl.ds((2 * block + side) * LANES, LANES)
            out_ref[:, lanes] = total_ref[pl.ds(side * BLOCKS + block, 6, stride=2 * BLOCKS), :]


CODES = ((SIDE + 1) * SIDE * SIDE, LANES)
ACC = (2 * ROWS * APITCH, LANES)
COLB = (2 * (COLS + 1) * KPITCH, LANES)
COLF = (2 * (COLS + 1) * FPITCH, LANES)


def array(shape, dtype=jnp.float32):
    return jax.ShapeDtypeStruct(shape, dtype)


def call(kernel, name, out, inputs, scratch=(), flops=0, hbm=False, limit=VMEM_LIMIT):
    vmem = pl.BlockSpec(memory_space=pltpu.VMEM)
    given = pl.BlockSpec(memory_space=pl.ANY) if hbm else vmem
    return pl.pallas_call(
        kernel,
        out_shape=out,
        in_specs=[given] * len(inputs),
        out_specs=jax.tree.map(lambda _: vmem, out),
        scratch_shapes=list(scratch),
        compiler_params=pltpu.CompilerParams(vmem_limit_bytes=limit),
        cost_estimate=pl.CostEstimate(flops=flops, bytes_accessed=1 << 20, transcendentals=0) if flops else None,
        name=name,
    )(*inputs)


def tiles(along, near, far, across):
    scratch = [
        pltpu.VMEM(CODES, jnp.int32),
        pltpu.VMEM(COLB, jnp.float32),
        pltpu.VMEM(COLF, jnp.float32),
        pltpu.VMEM((2 * ROWS * KPITCH, LANES), jnp.float32),
        pltpu.VMEM((ROWS, KEXP, B), jnp.bfloat16),
        pltpu.VMEM(ACC, jnp.float32),
        pltpu.SMEM(CODES, jnp.int32),
        pltpu.SMEM((SIDE * SIDE * 512 + 128,), jnp.int32),
        pltpu.SemaphoreType.DMA,
    ]
    out = (array((PART, LANES)),) * SIDE
    return call(tile_kernel, "tile_gradients", out, (*along, near, far, *across), scratch, flops=10**10)


def per_device(source, target, tile_pairs, tile_counts):
    groups = lax.axis_size("bundle")
    chips = groups // 2
    within = [(g, g ^ 1) for g in range(groups)]
    between = [(2 * z + 1, 2 * z + 2) for z in range(chips - 1)] + [(2 * z + 2, 2 * z + 1) for z in range(chips - 1)]

    def along_x(step):
        return [(SIDE * x + y, SIDE * ((x + step) % SIDE) + y) for x in range(SIDE) for y in range(SIDE)]

    def along_y(step):
        return [(SIDE * x + y, SIDE * x + (y + step) % SIDE) for x in range(SIDE) for y in range(SIDE)]

    slots = tile_pairs.shape[0]
    scratch = [
        pltpu.SMEM(tile_counts.shape, jnp.int32),
        pltpu.VMEM((2, slots), jnp.int32),
        pltpu.VMEM(source.shape, jnp.float32),
        pltpu.VMEM(target.shape, jnp.float32),
        pltpu.SemaphoreType.DMA((4,)),
    ]
    send = call(
        pack_kernel, "sort_and_pack", array((PAYLOAD, LANES)), (tile_counts, tile_pairs.T, source, target),
        scratch, hbm=True, limit=PACK_LIMIT,
    )
    passed = {step: lax.ppermute(send, "shard", along_x(step)) for step in FARTHEST_FIRST}
    along = (call(keep_kernel, "keep", array((PAYLOAD, LANES)), (send,), flops=10**9), passed[1], passed[2], passed[3])
    shared, across = call(split_kernel, "split", (array((SIDE * PART, LANES)), array((ACROSS, LANES))), along)
    near = lax.ppermute(shared, "bundle", within)
    far = lax.ppermute(shared, "bundle", between)
    passed = {step: lax.ppermute(across, "shard", along_y(step)) for step in FARTHEST_FIRST}
    parts = tiles(along, near, far, (across, passed[1], passed[2], passed[3]))
    back = [lax.ppermute(parts[step], "shard", along_y(-step)) for step in FARTHEST_FIRST]
    return call(
        sum_kernel, "add_parts", array((6, 8 * B)), (parts[0], *back), [pltpu.VMEM((PART, LANES), jnp.float32)]
    )


def solution(mesh):
    in_specs = (
        P(None, ("bundle", "shard")),
        P(None, ("bundle", "shard")),
        P(("bundle", "shard"), None),
        P(("bundle", "shard")),
    )
    out_specs = P(None, ("bundle", "shard"))
    return jax.shard_map(
        per_device, mesh=mesh, in_specs=in_specs, out_specs=out_specs, check_vma=False
    )
```
